256 devices in a mesh: walk: 16 (over y, z_hi, core), chol: 16 (over z_lo, x).
Axes of the slice: x: 4, y: 4, z: 8 (z_hi: 2, z_lo: 4; z = z_hi * 4 + z_lo), core: 2. Of those that a mesh axis runs over, the one named last changes fastest.
Arguments:
- greens: bfloat16 [512, 2, 100, 1000], P(('walk', 'chol')), may hold values from -6 to 6
- cholesky: bfloat16 [176, 2, 100, 1000], P('chol'), may hold values from -0.013671875 to 0.013671875
- fields: float32 [512, 176], P(('walk', 'chol')), may hold values from -6 to 6
- log_weight: float32 [512], P(('walk', 'chol')), may hold values from -4 to 4
- group_of: int32 [512], P(('walk', 'chol')), may hold values from 0 to 15
Outputs:
- force_bias: float32 [512, 176], P(('walk', 'chol'))
- e_coulomb: float32 [512], P(('walk', 'chol'))
- e_exchange: float32 [512], P(('walk', 'chol'))
- new_log_weight: float32 [512], P(('walk', 'chol'))
- group_share: float32 [16], replicated
The draws below stay inside these ranges and needn't reach their ends.
All inputs are finite; a program needn't handle non-finite values.
Results may differ from the reference program's by a relative error of at most 0.0003.
Values may be sent and summed in bfloat16 or wider, within the bound.
A program may use at most 192 MiB of HBM per device.

```python
import jax
import jax.numpy as jnp
from jax import lax

NOCC = 100
NORB = 1000
GROUPS = 16
CHOL = 176
WALKERS = 512


def with_ends(result, rng, least, high):
    spot = [jax.random.randint(jax.random.fold_in(rng, axis), (), 0, length) for axis, length in enumerate(result.shape)]
    main_axis = result.shape.index(max(result.shape))
    beside = spot[:main_axis] + [(spot[main_axis] + 1) % result.shape[main_axis]] + spot[main_axis + 1:]
    return result.at[tuple(spot)].set(least).at[tuple(beside)].set(high)


def block_scale(stream_key, extent, pieces, smallest, largest):
    gain, own = 1.0, jax.random.fold_in(stream_key, 6)
    for dim, shards_of in pieces:
        draws = jnp.exp(jax.random.uniform(jax.random.fold_in(own, dim), (shards_of,), jnp.float32, smallest / len(pieces), largest / len(pieces)))
        gain = gain * jnp.repeat(draws, extent[dim] // shards_of).reshape([-1 if axis == dim else 1 for axis in range(len(extent))])
    return gain


def normal_values(own_key, dims, width, reach, shards=(), held_as=jnp.bfloat16):
    array = width * jax.random.normal(own_key, dims, jnp.float32)
    if shards:
        array = array * block_scale(own_key, dims, shards, -0.22, 0.18)
    return jnp.clip(array, -reach, reach).astype(held_as)


def setup_inputs(seed: int = 0) -> dict:
    splits = jax.random.split(jax.random.key(seed), 6)
    return {
        "greens": normal_values(splits[0], (WALKERS, 2, NOCC, NORB), 1.0, 6.0, ((0, 256),)),
        "cholesky": normal_values(splits[1], (CHOL, 2, NOCC, NORB), (2 * NOCC * NORB) ** -0.5, 0.013671875, ((0, 16),)),
        "fields": normal_values(splits[2], (WALKERS, CHOL), 1.0, 6.0, ((0, 256),), jnp.float32),
        "log_weight": normal_values(splits[3], (WALKERS,), 1.0, 4.0, ((0, 256),), jnp.float32),
        "group_of": with_ends(jax.random.randint(splits[4], (WALKERS,), 0, GROUPS), jax.random.fold_in(splits[4], 1), 0, GROUPS - 1).astype(jnp.int32),
    }


def reference(greens, cholesky, fields, log_weight, group_of):
    chol_wide = cholesky.astype(jnp.float32)

    def walker_terms(green_one):
        prods = jnp.einsum('gsip,sjp->gsij', chol_wide, green_one.astype(jnp.float32), precision=lax.Precision.HIGHEST)
        bias = jnp.einsum('gsii->g', prods)
        exch = jnp.einsum('gsij,gsji->', prods, prods)
        return (bias, exch)
    force_bias, exch_sum = lax.map(walker_terms, greens)
    root = jnp.sqrt(jnp.float32(CHOL))
    e_coulomb = lax.optimization_barrier(jnp.sum(force_bias * force_bias, axis=1)) / (2.0 * root)
    e_exchange = -exch_sum / (2.0 * root)
    importance = lax.optimization_barrier(jnp.sum(fields * force_bias - 0.5 * force_bias * force_bias, axis=1)) / root
    new_log_weight = log_weight + importance - e_coulomb - e_exchange
    onehot = (group_of[:, None] == jnp.arange(GROUPS, dtype=jnp.int32)[None, :]).astype(jnp.float32)
    group_sums = jnp.dot(jnp.exp(new_log_weight), onehot, precision=lax.Precision.HIGHEST)
    group_share = GROUPS * group_sums / jnp.sum(group_sums)
    return (force_bias, e_coulomb, e_exchange, new_log_weight, group_share)
```

```python
import functools

import jax
import jax.numpy as jnp
import numpy as np
from jax import lax
from jax.experimental import pallas as pl
from jax.experimental.pallas import tpu as pltpu
from jax.sharding import PartitionSpec as P

GROUPS = 16
ROWS = 112
MESH = pl.DeviceIdType.MESH
HIGHEST = lax.Precision.HIGHEST

SLOTS = ((0, 0), (1, 0), (0, -1), (0, 1), (1, -1), (1, 1), (0, 2), (1, -2))


def device(x, y, z, core):
    return {"walk": (y * 2 + lax.div(z, 4)) * 2 + core, "chol": lax.rem(z, 4) * 4 + x}


def kernel(
    greens, cholesky, fields, log_weight, group_of,
    bias_out, coulomb_out, exchange_out, weight_out, share_out,
    slabs, walkers, c_pad, g_pad, prods_a, prods_b, bias_rows, exch,
    back, back_in, combined, stage_out, stage_in,
    local_sem, c_send, c_recv, g_send, g_recv, b_send, b_recv, s_send, s_recv,
):
    wi, ci = lax.axis_index("walk"), lax.axis_index("chol")
    core = lax.rem(wi, 2)
    y = lax.div(wi, 4)
    z_lo = lax.div(ci, 4)
    z = lax.rem(lax.div(wi, 2), 2) * 4 + z_lo
    x = lax.rem(ci, 4)
    spin = lax.div(y, 2)
    mate = 3 - y
    step = 1 - 2 * core

    def at_x(offset):
        return lax.rem(x + offset + 4, 4)

    def at_z(offset):
        return lax.rem(z + offset + 8, 8)

    def stage_peer(stage, r):
        if stage == 0:
            p = lax.rem(y * 4 + x + r, 16)
            return device(lax.rem(p, 4), lax.div(p, 4), z, core)
        p = lax.rem(z * 2 + core + r, 16)
        return device(x, y, lax.div(p, 2), lax.rem(p, 2))

    own_c = pltpu.make_async_copy(cholesky.at[:, spin], slabs.at[pl.ds(x * 11, 11)], local_sem.at[0])
    own_g = pltpu.make_async_copy(greens.at[:, spin], walkers.at[0], local_sem.at[1])
    own_g.start()
    own_c.start()

    barrier = pltpu.get_barrier_semaphore()

    def greet(peer):
        pl.semaphore_signal(barrier, inc=1, device_id=peer, device_id_type=MESH)

    for stage in range(2):
        def greet_stage(r, _, stage=stage):
            greet(stage_peer(stage, r))
            return 0
        lax.fori_loop(1, 16, greet_stage, 0)
    for offset in (-2, -1, 1, 2):
        greet(device(x, mate, at_z(offset), core))
    pl.semaphore_wait(barrier, 34)

    first_a, first_b = 6 * core, 6 * core + 3 + 0 * core
    parts = {"a": (first_a, 3), "b": (first_b, 2), "m": (5, 1)}
    c_copies = {}

    def c_copy(index, src, slab, part, peer):
        first, count = parts[part]
        place = slabs.at[pl.ds(slab * 11 + first, count)]
        if src is None:
            src = cholesky.at[pl.ds(first, count), spin]
        else:
            src = place
        return pltpu.make_async_remote_copy(
            src_ref=src, dst_ref=place, send_sem=c_send.at[index], recv_sem=c_recv.at[index],
            device_id=peer, device_id_type=MESH,
        )

    ahead, behind = at_x(step), at_x(-step)
    to_ahead, to_behind = device(ahead, y, z, core), device(behind, y, z, core)
    sibling = device(x, y, z, 1 - core)
    opposite = at_x(2)
    direct = [
        c_copy(0, None, x, "a", to_ahead),
        c_copy(3, None, x, "b", to_behind),
        c_copy(1, None, x, "b", to_ahead),
        c_copy(4, None, x, "a", to_behind),
        c_copy(2, None, x, "m", to_ahead),
    ]
    relay = {
        5: c_copy(5, 1, behind, "a", to_ahead),
        6: c_copy(6, 1, ahead, "b", to_behind),
        7: c_copy(7, 1, behind, "m", to_ahead),
    }
    landed = {0: (behind, "a"), 1: (behind, "b"), 2: (behind, "m"), 3: (ahead, "b"), 4: (ahead, "a"),
              5: (opposite, "a"), 6: (opposite, "b"), 7: (opposite, "m")}
    arrive = {i: c_copy(i, 1, slab, part, to_ahead) for i, (slab, part) in landed.items()}
    share = {i: c_copy(8 + i, 1, slab, part, sibling) for i, (slab, part) in landed.items()}

    their = {"a": (6 - first_a, 3), "b": (9 - first_a, 2), "m": (5, 1)}

    def from_sibling(i):
        slab, part = landed[i]
        if i < 5:
            slab = ahead if i < 3 else behind
        first, count = their[part]
        place = slabs.at[pl.ds(slab * 11 + first, count)]
        return pltpu.make_async_remote_copy(
            src_ref=place, dst_ref=place, send_sem=c_send.at[8 + i], recv_sem=c_recv.at[8 + i],
            device_id=sibling, device_id_type=MESH,
        )

    def g_copy(index, src, slot, peer):
        return pltpu.make_async_remote_copy(
            src_ref=src, dst_ref=walkers.at[slot], send_sem=g_send.at[index], recv_sem=g_recv.at[slot],
            device_id=peer, device_id_type=MESH,
        )

    own_planes, other_planes = greens.at[:, spin], greens.at[:, 1 - spin]
    g_copies = [
        g_copy(0, other_planes, 1, device(x, mate, z, core)),
        g_copy(1, own_planes, 2, device(x, y, at_z(1), core)),
        g_copy(2, own_planes, 3, device(x, y, at_z(-1), core)),
        g_copy(3, own_planes, 6, device(x, y, at_z(-2), core)),
        g_copy(4, walkers.at[1], 4, device(x, y, at_z(1), core)),
        g_copy(5, walkers.at[1], 5, device(x, y, at_z(-1), core)),
        g_copy(6, walkers.at[1], 7, device(x, y, at_z(2), core)),
    ]

    def g_wait(slot):
        g_copy(0, walkers.at[slot], slot, sibling).wait_recv()

    g_copies[0].start()
    for copy in direct[:2]:
        copy.start()
    for copy in g_copies[1:3]:
        copy.start()
    for copy in direct[2:]:
        copy.start()
    g_copies[3].start()

    zero = jnp.zeros((ROWS, 1024), jnp.bfloat16)

    def clear_c(i, _):
        c_pad[pl.ds(i * ROWS, ROWS), :] = zero
        return 0

    def clear_g(i, _):
        g_pad[i] = jnp.zeros((128, 1024), jnp.bfloat16)
        bias_rows[i] = jnp.zeros((128, 128), jnp.float32)
        exch[i] = jnp.zeros((8, 128), jnp.float32)
        return 0

    lax.fori_loop(0, 44, clear_c, 0)
    lax.fori_loop(0, 16, clear_g, 0)

    def pack_slab(slab):
        def one(i, _):
            g = slab * 11 + i
            c_pad[pl.ds(g * ROWS, 100), 0:1000] = slabs[g]
            return 0
        lax.fori_loop(0, 11, one, 0)

    def pack_walkers(slot):
        for i in range(2):
            g_pad[slot * 2 + i, 0:100, 0:1000] = walkers[slot, i]

    row = lax.broadcasted_iota(jnp.int32, (104, 128), 0)
    col = lax.broadcasted_iota(jnp.int32, (104, 128), 1)
    diagonal = row == col

    def slab_of(task):
        q = lax.div(task, 8)
        return lax.rem(x + jnp.where(q == 2, 3, jnp.where(q == 3, 2, q)), 4)

    def product(task, buf):
        slot = lax.rem(task, 8)
        lhs = c_pad[pl.ds(slab_of(task) * (11 * ROWS), 11 * ROWS), :]
        rhs = g_pad[pl.ds(slot * 2, 2)].reshape(256, 1024)
        buf[...] = lax.dot_general(lhs, rhs, (((1,), (1,)), ((), ())), preferred_element_type=jnp.float32)

    def reduce(task, buf):
        slot = lax.rem(task, 8)
        first = slab_of(task) * 11
        for h in range(2):
            total = None
            for g in range(11):
                p = buf[g * ROWS : (g + 1) * ROWS, h * 128 : (h + 1) * 128]
                turned = p.T
                q = p[:104, :ROWS] * turned[:104, :]
                part = jnp.sum(q.reshape(13, 8, ROWS), axis=0)
                total = part if total is None else total + part
                d = jnp.sum(jnp.where(diagonal, p[:104], 0.0).reshape(13, 8, 128), axis=0)
                bias_rows[slot * 2 + h, pl.ds(first + g, 1), :] = jnp.sum(d, axis=0, keepdims=True)
            exch[slot * 2 + h, :, 0:ROWS] += total

    def events(k):
        @pl.when(k == 0)
        def _():
            own_c.wait()
            own_g.wait()
            pack_slab(x)
            pack_walkers(0)
            g_wait(1)
            for copy in g_copies[4:]:
                copy.start()
            pack_walkers(1)

        @pl.when(k == 1)
        def _():
            g_wait(2)
            g_wait(3)
            pack_walkers(2)
            pack_walkers(3)
            arrive[3].wait_recv()
            relay[6].start()
            share[3].start()
            arrive[0].wait_recv()
            relay[5].start()
            share[0].start()

        @pl.when(k == 2)
        def _():
            g_wait(4)
            g_wait(5)
            pack_walkers(4)
            pack_walkers(5)
            for i in (1, 4):
                arrive[i].wait_recv()
                share[i].start()

        @pl.when(k == 3)
        def _():
            g_wait(6)
            g_wait(7)
            pack_walkers(6)
            pack_walkers(7)
            arrive[2].wait_recv()
            share[2].start()

            @pl.when(core == 0)
            def _():
                relay[7].start()

        @pl.when(k == 4)
        def _():
            for i in range(5):
                from_sibling(i).wait_recv()
            pack_slab(at_x(1))

        @pl.when(k == 8)
        def _():
            pack_slab(at_x(3))

        @pl.when(k == 10)
        def _():
            for i in (6, 5):
                arrive[i].wait_recv()
                share[i].start()

            @pl.when(core == 0)
            def _():
                arrive[7].wait_recv()
                share[7].start()

        @pl.when(k == 12)
        def _():
            for i in (6, 5):
                from_sibling(i).wait_recv()

            @pl.when(core == 1)
            def _():
                from_sibling(7).wait_recv()
            pack_slab(opposite)

    prods_b[...] = jnp.zeros_like(prods_b)

    def body(k, _):
        events(k)
        product(2 * k, prods_a)

        reduce(jnp.maximum(2 * k - 1, 0), prods_b)
        product(2 * k + 1, prods_b)
        reduce(2 * k, prods_a)
        return 0

    lax.fori_loop(0, 16, body, 0)
    reduce(jnp.int32(31), prods_b)

    for w in range(16):
        bias_rows[w, 44:45, :] = jnp.sum(exch[w], axis=0, keepdims=True)
    ones = jnp.ones((8, 128), jnp.float32)
    sums = lax.dot_general(
        ones, bias_rows[...].reshape(16 * 128, 128), (((1,), (1,)), ((), ())),
        precision=HIGHEST, preferred_element_type=jnp.float32,
    )
    for slot in range(8):
        back[slot] = sums[:, slot * 256 : (slot + 1) * 256]
    returns = []
    for slot, (other, offset) in enumerate(SLOTS):
        if slot:
            copy = pltpu.make_async_remote_copy(
                src_ref=back.at[slot], dst_ref=back_in.at[slot], send_sem=b_send.at[slot], recv_sem=b_recv.at[slot],
                device_id=device(x, mate if other else y, at_z(offset), core), device_id_type=MESH,
            )
            copy.start()
            returns.append(copy)
    for copy in returns:
        copy.wait_recv()
    own = back[0]
    for quarter, (s, t) in enumerate(((0, 1), (3, 5), (6, 7), (2, 4))):
        combined[quarter] = (own if s == 0 else back_in[s]) + back_in[t]
    lane = lax.broadcasted_iota(jnp.int32, (8, 128), 1)
    bias, exch_sum = [], []
    for w in range(2):
        spread, total = None, None
        for m in range(4):
            block = combined[lax.rem(z_lo - m + 4, 4), :, w * 128 : (w + 1) * 128]
            energy = jnp.sum(jnp.where(lane == 44, block, 0.0), axis=1, keepdims=True)
            wide = jnp.concatenate([jnp.where(lane < 44, block, 0.0), jnp.zeros((8, 128), jnp.float32)], axis=1)
            if m:
                wide = pltpu.roll(wide, 44 * m, 1)
            spread = wide if spread is None else spread + wide
            total = energy if total is None else total + energy
        bias.append(spread)
        exch_sum.append(total)
    top = lax.broadcasted_iota(jnp.int32, (8, 256), 0) == 0
    bias = jnp.where(top, bias[0], bias[1])[0:2, 0:176]
    first = lax.broadcasted_iota(jnp.int32, (2, 1), 0) == 0
    exch_sum = jnp.where(first, exch_sum[0][0:2], exch_sum[1][0:2])
    root = np.sqrt(np.float32(176))
    bias_out[...] = bias
    coulomb = jnp.sum(bias * bias, axis=1, keepdims=True) / (2.0 * root)
    exchange = -exch_sum / (2.0 * root)
    importance = jnp.sum(fields[...] * bias - 0.5 * bias * bias, axis=1, keepdims=True) / root
    weight = jnp.where(first, log_weight[0], log_weight[1]) + importance - coulomb - exchange
    member = lax.broadcasted_iota(jnp.int32, (2, 128), 1) == jnp.where(
        lax.broadcasted_iota(jnp.int32, (2, 128), 0) == 0, group_of[0], group_of[1]
    )
    group = jnp.sum(jnp.where(member, jnp.exp(weight), 0.0), axis=0, keepdims=True)

    for stage in range(2):
        me = y * 4 + x if stage == 0 else z * 2 + core
        group = jnp.broadcast_to(group, (8, 128))
        stage_out[stage] = group
        stage_in[stage, 0] = group

        def send(r, _, stage=stage):
            pltpu.make_async_remote_copy(
                src_ref=stage_out.at[stage], dst_ref=stage_in.at[stage, r],
                send_sem=s_send.at[stage], recv_sem=s_recv.at[stage],
                device_id=stage_peer(stage, r), device_id_type=MESH,
            ).start()
            return 0

        lax.fori_loop(1, 16, send, 0)
        if stage == 0:
            for w in range(2):
                coulomb_out[w] = jnp.sum(coulomb[w : w + 1])
                exchange_out[w] = jnp.sum(exchange[w : w + 1])
                weight_out[w] = jnp.sum(weight[w : w + 1])
        everyone = stage_in.at[stage, pl.ds(1, 15)]
        whole = pltpu.make_async_remote_copy(
            src_ref=everyone, dst_ref=everyone, send_sem=s_send.at[stage], recv_sem=s_recv.at[stage],
            device_id=sibling, device_id_type=MESH,
        )
        whole.wait_recv()
        whole.wait_send()
        group = None
        for a in range(16):
            term = stage_in[stage, lax.rem(me - a + 16, 16), 0:1, :]
            group = term if group is None else group + term
    share_out[...] = (GROUPS * group / jnp.sum(group, axis=1, keepdims=True))[:, 0:GROUPS]

    for copy in direct:
        copy.wait_send()
    for i in (5, 6):
        relay[i].wait_send()
    for i in range(7):
        share[i].wait_send()

    @pl.when(core == 0)
    def _():
        relay[7].wait_send()
        share[7].wait_send()

    for copy in g_copies:
        copy.wait_send()
    for copy in returns:
        copy.wait_send()


def local(greens, cholesky, fields, log_weight, group_of):
    f32, bf16 = jnp.float32, jnp.bfloat16
    dma = pltpu.SemaphoreType.DMA
    vmem = pl.BlockSpec(memory_space=pltpu.VMEM)
    smem = pl.BlockSpec(memory_space=pltpu.SMEM)
    hbm = pl.BlockSpec(memory_space=pl.ANY)
    bias, coulomb, exchange, weight, share = pl.pallas_call(
        kernel,
        out_shape=[
            jax.ShapeDtypeStruct((2, 176), f32),
            jax.ShapeDtypeStruct((2,), f32),
            jax.ShapeDtypeStruct((2,), f32),
            jax.ShapeDtypeStruct((2,), f32),
            jax.ShapeDtypeStruct((1, GROUPS), f32),
        ],
        in_specs=[hbm, hbm, vmem, smem, smem],
        out_specs=[vmem, smem, smem, smem, vmem],
        scratch_shapes=[
            pltpu.VMEM((44, 100, 1000), bf16),
            pltpu.VMEM((8, 2, 100, 1000), bf16),
            pltpu.VMEM((44 * ROWS, 1024), bf16),
            pltpu.VMEM((16, 128, 1024), bf16),
            pltpu.VMEM((11 * ROWS, 256), f32),
            pltpu.VMEM((11 * ROWS, 256), f32),
            pltpu.VMEM((16, 128, 128), f32),
            pltpu.VMEM((16, 8, 128), f32),
            pltpu.VMEM((8, 8, 256), f32),
            pltpu.VMEM((8, 8, 256), f32),
            pltpu.VMEM((4, 8, 256), f32),
            pltpu.VMEM((2, 8, 128), f32),
            pltpu.VMEM((2, 16, 8, 128), f32),
            dma((2,)),
            dma((16,)),
            dma((16,)),
            dma((7,)),
            dma((8,)),
            dma((8,)),
            dma((8,)),
            dma((2,)),
            dma((2,)),
        ],
        compiler_params=pltpu.CompilerParams(
            collective_id=0, has_side_effects=True, vmem_limit_bytes=56 * 2**20
        ),
        cost_estimate=pl.CostEstimate(flops=14_080_000_000, bytes_accessed=6_000_000, transcendentals=256),
    )(greens, cholesky, fields, log_weight, group_of)
    return bias, coulomb, exchange, weight, share.reshape(GROUPS)


def solution(mesh):
    in_specs = (
        P(("walk", "chol"), None, None, None),
        P("chol", None, None, None),
        P(("walk", "chol"), None),
        P(("walk", "chol")),
        P(("walk", "chol")),
    )
    out_specs = (
        P(("walk", "chol"), None),
        P(("walk", "chol")),
        P(("walk", "chol")),
        P(("walk", "chol")),
        P(),
    )
    return jax.shard_map(local, mesh=mesh, in_specs=in_specs, out_specs=out_specs, check_vma=False)
```

```python
import jax
import jax.numpy as jnp
import numpy as np
from jax import lax
from jax.experimental import pallas as pl
from jax.experimental.pallas import tpu as pltpu
from jax.sharding import PartitionSpec as P

GROUPS = 16
ROWS = 104
BLOCK = 11
MESH = pl.DeviceIdType.MESH
HIGHEST = lax.Precision.HIGHEST

SLOTS = ((0, 0), (1, 0), (0, -1), (0, 1), (1, -1), (0, 2), (1, 1), (1, -2))
WALKERS = (
    (0, 0), (0, 1), (1, 0), (2, 0), (3, 0), (1, 1), (2, 1), (3, 1),
    (4, 0), (5, 0), (4, 1), (5, 1), (6, 0), (7, 0), (6, 1), (7, 1),
)
QUARTERS = ((0, 1), (3, 6), (5, 7), (2, 4))

STEPS = (
    ((-1, 0), (1, 2)),
    ((-1, 1), (1, 3)),
    ((2, 0), (2, 2)),
    ((2, 1), (1, 0)),
    ((-1, 2), (1, 1)),
    ((-1, 3), (2, 3)),
)
ACROSS = ((0, 0), (0, 1), (1, 0), (2, 0), (2, 1), (3, 0), (3, 1), (4, 0), (4, 1))


def device(x, y, z, core):
    return {"walk": (y * 2 + lax.div(z, 4)) * 2 + core, "chol": lax.rem(z, 4) * 4 + x}


def kernel(
    greens, cholesky, fields, log_weight, group_of,
    bias_out, scalars_out, share_out,
    planes, walkers, prods_a, prods_b, bias_rows, exch, order,
    back, back_in, combined, stage_out, stage_in,
    local_sem, x_send, x_recv, near_send, near_recv, y_send, y_recv, far_recv,
    g_send, g_recv, b_send, b_recv, s_send, s_recv,
):
    wi, ci = lax.axis_index("walk"), lax.axis_index("chol")
    core = lax.rem(wi, 2)
    y = lax.div(wi, 4)
    z_lo = lax.div(ci, 4)
    z = lax.rem(lax.div(wi, 2), 2) * 4 + z_lo
    x = lax.rem(ci, 4)
    spin = lax.div(y, 2)
    mate = 3 - y
    odd = lax.rem(y, 2)
    neighbour = y + 1 - 2 * odd
    sends_across = core == odd

    def at_x(offset):
        return lax.rem(x + offset + 4, 4)

    def at_z(offset):
        return lax.rem(z + offset + 8, 8)

    def stage_peer(stage, r):
        if stage == 0:
            p = lax.rem(y * 4 + x + r, 16)
            return device(lax.rem(p, 4), lax.div(p, 4), z, core)
        p = lax.rem(z * 2 + core + r, 16)
        return device(x, y, lax.div(p, 2), lax.rem(p, 2))

    own_c = pltpu.make_async_copy(cholesky.at[:, spin], planes.at[pl.ds(0, 11)], local_sem.at[0])
    own_g = pltpu.make_async_copy(greens.at[:, spin], walkers.at[pl.ds(0, 2)], local_sem.at[1])
    own_g.start()
    own_c.start()

    barrier = pltpu.get_barrier_semaphore()

    def greet(peer):
        pl.semaphore_signal(barrier, inc=1, device_id=peer, device_id_type=MESH)

    for stage in range(2):
        def greet_stage(r, _, stage=stage):
            greet(stage_peer(stage, r))
            return 0
        lax.fori_loop(1, 16, greet_stage, 0)
    for offset in (-2, -1, 1, 2):
        greet(device(x, mate, at_z(offset), core))

    def plane_of(i, c):
        first = 3 * odd + 4 * c
        return first + odd + i if i < 3 else first + 3 * (1 - odd)

    def place(step, side, c):
        return BLOCK * (1 + step // 2) + (step % 2) * 4 + side * 2 + c

    def across_place(n):
        return BLOCK * (1 + n // 3) + 8 + n % 3

    lanes = lax.broadcasted_iota(jnp.int32, (1, 128), 1)
    rows = [(i, x * 11 + i) for i in range(11)]
    for step in range(6):
        for side in range(2):
            home, i = STEPS[step][side]
            for c in range(2):
                rows.append((place(step, side, c), at_x(home) * 11 + plane_of(i, c)))
    for n, (step, side) in enumerate(ACROSS):
        home, i = STEPS[step][side]
        rows.append((across_place(n), at_x(home) * 11 + 8 * (1 - odd) + i))
    rows.append((44, 44))
    order[...] = jnp.zeros_like(order)
    for at, row in rows:
        order[at : at + 1, :] = (lanes == row).astype(jnp.float32)
    bias_rows[...] = jnp.zeros_like(bias_rows)
    exch[...] = jnp.zeros_like(exch)
    prods_b[...] = jnp.zeros_like(prods_b)
    back[...] = jnp.zeros_like(back)
    pl.semaphore_wait(barrier, 34)

    sibling = device(x, y, z, 1 - core)
    to_side = (device(at_x(1), y, z, core), device(at_x(-1), y, z, core))

    def x_copy(step, side):
        home, i = STEPS[step][side]
        if home == 2:
            before = STEPS.index(next(s for s in STEPS if s[side] == ((-1, 1)[side], i)))
            src = planes.at[place(before, side, core)]
        else:
            src = cholesky.at[plane_of(i, core), spin]
        return pltpu.make_async_remote_copy(
            src_ref=src, dst_ref=planes.at[place(step, side, core)],
            send_sem=x_send.at[step, side], recv_sem=x_recv.at[step, side],
            device_id=to_side[side], device_id_type=MESH,
        )

    def near_copy(step, side, c):
        ref = planes.at[place(step, side, c)]
        return pltpu.make_async_remote_copy(
            src_ref=ref, dst_ref=ref, send_sem=near_send.at[step, side], recv_sem=near_recv.at[step, side],
            device_id=sibling, device_id_type=MESH,
        )

    def across_copy(n):
        step, side = ACROSS[n]
        return pltpu.make_async_remote_copy(
            src_ref=planes.at[place(step, side, core)], dst_ref=planes.at[across_place(n)],
            send_sem=y_send.at[n], recv_sem=y_recv.at[n],
            device_id=device(x, neighbour, z, core), device_id_type=MESH,
        )

    def onward_copy(n):
        ref = planes.at[across_place(n)]
        return pltpu.make_async_remote_copy(
            src_ref=ref, dst_ref=ref, send_sem=y_send.at[n], recv_sem=far_recv.at[n],
            device_id=sibling, device_id_type=MESH,
        )

    up, down = device(x, y, at_z(1), core), device(x, y, at_z(-1), core)

    def g_copy(slot, h):
        if slot < 4:
            src = greens.at[h, 1 - spin if slot == 1 else spin]
        else:
            src = walkers.at[WALKERS.index(({4: 1, 5: 3, 6: 1, 7: 4}[slot], h))]
        peer = device(x, mate, z, core) if slot == 1 else up if slot in (2, 4, 7) else down
        return pltpu.make_async_remote_copy(
            src_ref=src, dst_ref=walkers.at[WALKERS.index((slot, h))],
            send_sem=g_send.at[slot, h], recv_sem=g_recv.at[slot, h],
            device_id=peer, device_id_type=MESH,
        )

    def x_start(step):
        for side in range(2):
            x_copy(step, side).start()

    def x_arrived(step):
        for side in range(2):
            x_copy(step, side).wait_recv()
            near_copy(step, side, core).start()

        @pl.when(sends_across)
        def _():
            for n, (s, _side) in enumerate(ACROSS):
                if s == step:
                    across_copy(n).start()

    def across_arrived(numbers):
        @pl.when(jnp.logical_not(sends_across))
        def _():
            for n in numbers:
                across_copy(n).wait_recv()
                onward_copy(n).start()

    def block_whole(block):
        for step in (2 * block - 2, 2 * block - 1):
            for side in range(2):
                near_copy(step, side, 1 - core).wait_recv()

        @pl.when(sends_across)
        def _():
            for n in range(3 * block - 3, 3 * block):
                onward_copy(n).wait_recv()

    for step in range(2):
        g_copy(1, step).start()
        x_start(step)
        g_copy(2, step).start()
        g_copy(3, step).start()
    own_c.wait()
    own_g.wait()

    row = lax.broadcasted_iota(jnp.int32, (ROWS, 128), 0)
    col = lax.broadcasted_iota(jnp.int32, (ROWS, 128), 1)
    diagonal = row == col
    gap = jnp.zeros((28, 1000), jnp.bfloat16)

    def block_of(t):
        late = jnp.where(t < 18, 2, jnp.where(t < 24, lax.rem(t - 18, 3), 3))
        return jnp.where(t < 4, 0, jnp.where(t < 8, 1, jnp.where(t < 12, lax.rem(t, 2), late)))

    def pair_of(t):
        late = jnp.where(t < 18, t - 12, jnp.where(t < 24, 6 + lax.div(t - 18, 3), t - 24))
        return jnp.where(t < 4, t, jnp.where(t < 8, t - 4, jnp.where(t < 12, 4 + lax.div(t - 8, 2), late)))

    def product(t, buf):
        first, pair = block_of(t) * BLOCK, pair_of(t) * 2
        lhs = [part for i in range(BLOCK) for part in (planes[first + i], gap[: ROWS - 100])]
        rhs = [walkers[pair], gap, walkers[pair + 1], gap]
        buf[...] = lax.dot_general(
            jnp.concatenate(lhs, axis=0), jnp.concatenate(rhs, axis=0), (((1,), (1,)), ((), ())),
            preferred_element_type=jnp.float32,
        )

    def reduce(t, buf):
        first, pair = block_of(t) * BLOCK, pair_of(t) * 2
        for h in range(2):
            total = None
            for g in range(BLOCK):
                p = buf[g * ROWS : (g + 1) * ROWS, h * 128 : (h + 1) * 128]
                turned = p.T
                q = p[:, :ROWS] * turned[:ROWS, :]
                part = jnp.sum(q.reshape(ROWS // 8, 8, ROWS), axis=0)
                total = part if total is None else total + part
                d = jnp.sum(jnp.where(diagonal, p, 0.0).reshape(ROWS // 8, 8, 128), axis=0)
                bias_rows[pair + h, pl.ds(first + g, 1), :] = jnp.sum(d, axis=0, keepdims=True)
            exch[pair + h, :, 0:ROWS] += total

    def before(t, parity):
        def at(when, work):
            if when % 2 == parity:
                pl.when(t == when)(work)

        def walker(slot, h, *onward):
            g_copy(slot, h).wait_recv()
            for later in onward:
                g_copy(later, h).start()

        def first(h):
            x_arrived(h)
            x_start(h + 2)
            walker(3, h, 5)
            walker(1, h, 4)
            walker(2, h)

        def second():
            across_arrived((0, 1, 2))
            x_arrived(2)
            x_start(4)
            walker(4, 0, 7, 6)
            walker(5, 0)
            block_whole(1)

        def third():
            x_arrived(3)
            x_start(5)
            walker(4, 1, 7, 6)
            walker(5, 1)

        def fourth():
            across_arrived((3, 4, 5))
            block_whole(2)

        def fifth():
            walker(6, 0)
            walker(7, 0)

        def sixth():
            x_arrived(5)
            across_arrived((6, 7, 8))
            walker(6, 1)
            walker(7, 1)

        at(1, lambda: first(0))
        at(2, lambda: first(1))
        at(4, second)
        at(10, third)
        at(12, fourth)
        at(14, lambda: x_arrived(4))
        at(18, fifth)
        at(21, sixth)
        at(24, lambda: block_whole(3))

    def body(k, _):
        before(2 * k, 0)
        @pl.when(k>=0)
        def _():
            product(2 * k, prods_a)
            reduce(jnp.maximum(2 * k - 1, 0), prods_b)
        before(2 * k + 1, 1)
        @pl.when(k>=0)
        def _():
            product(2 * k + 1, prods_b)
            reduce(2 * k, prods_a)
        return 0

    lax.fori_loop(0, 16, body, 0)
    reduce(jnp.int32(31), prods_b)

    for w in range(16):
        bias_rows[w, 44:45, :] = jnp.sum(exch[w], axis=0, keepdims=True)
    sums = lax.dot_general(
        jnp.ones((8, 128), jnp.float32), bias_rows[...].reshape(16 * 128, 128), (((1,), (1,)), ((), ())),
        precision=HIGHEST, preferred_element_type=jnp.float32,
    )
    sums = jnp.concatenate([sums[0:1, w * 128 : (w + 1) * 128] for w in range(16)], axis=0)
    sums = jnp.dot(sums, order[...], precision=HIGHEST, preferred_element_type=jnp.float32)
    for slot in range(8):
        for h in range(2):
            w = WALKERS.index((slot, h))
            back[slot, h : h + 1] = sums[w : w + 1]
    returns = []
    for slot, (other, offset) in enumerate(SLOTS):
        if slot:
            copy = pltpu.make_async_remote_copy(
                src_ref=back.at[slot], dst_ref=back_in.at[slot], send_sem=b_send.at[slot], recv_sem=b_recv.at[slot],
                device_id=device(x, mate if other else y, at_z(offset), core), device_id_type=MESH,
            )
            copy.start()
            returns.append(copy)
    for copy in returns:
        copy.wait_recv()
    for quarter, (s, t) in enumerate(QUARTERS):
        combined[quarter] = (back[0] if s == 0 else back_in[s]) + back_in[t]
    lane = lax.broadcasted_iota(jnp.int32, (8, 128), 1)
    bias, exch_sum = None, None
    for m in range(4):
        block = combined[lax.rem(z_lo - m + 4, 4)]
        energy = jnp.sum(jnp.where(lane == 44, block, 0.0), axis=1, keepdims=True)
        wide = jnp.concatenate([jnp.where(lane < 44, block, 0.0), jnp.zeros((8, 128), jnp.float32)], axis=1)
        if m:
            wide = pltpu.roll(wide, 44 * m, 1)
        bias = wide if bias is None else bias + wide
        exch_sum = energy if exch_sum is None else exch_sum + energy
    bias, exch_sum = bias[0:2, 0:176], exch_sum[0:2]
    first = lax.broadcasted_iota(jnp.int32, (2, 1), 0) == 0
    root = np.sqrt(np.float32(176))
    coulomb = jnp.sum(bias * bias, axis=1, keepdims=True) / (2.0 * root)
    exchange = -exch_sum / (2.0 * root)
    importance = jnp.sum(fields[...] * bias - 0.5 * bias * bias, axis=1, keepdims=True) / root
    weight = jnp.where(first, log_weight[0], log_weight[1]) + importance - coulomb - exchange
    member = lax.broadcasted_iota(jnp.int32, (2, 128), 1) == jnp.where(
        lax.broadcasted_iota(jnp.int32, (2, 128), 0) == 0, group_of[0], group_of[1]
    )
    group = jnp.sum(jnp.where(member, jnp.exp(weight), 0.0), axis=0, keepdims=True)

    for stage in range(2):
        me = y * 4 + x if stage == 0 else z * 2 + core
        group = jnp.broadcast_to(group, (8, 128))
        stage_out[stage] = group
        stage_in[stage, 0] = group
        for r in range(1, 16):
            pltpu.make_async_remote_copy(
                src_ref=stage_out.at[stage], dst_ref=stage_in.at[stage, r],
                send_sem=s_send.at[stage], recv_sem=s_recv.at[stage],
                device_id=stage_peer(stage, r), device_id_type=MESH,
            ).start()
        if stage == 0:
            bias_out[...] = bias
            for w in range(2):
                scalars_out[w] = jnp.sum(coulomb[w : w + 1])
                scalars_out[2 + w] = jnp.sum(exchange[w : w + 1])
                scalars_out[4 + w] = jnp.sum(weight[w : w + 1])
        everyone = stage_in.at[stage, pl.ds(1, 15)]
        whole = pltpu.make_async_remote_copy(
            src_ref=everyone, dst_ref=everyone, send_sem=s_send.at[stage], recv_sem=s_recv.at[stage],
            device_id=sibling, device_id_type=MESH,
        )
        whole.wait_recv()
        whole.wait_send()
        group = None
        for a in range(16):
            term = stage_in[stage, lax.rem(me - a + 16, 16), 0:1, :]
            group = term if group is None else group + term
    share_out[...] = (GROUPS * group / jnp.sum(group, axis=1, keepdims=True))[:, 0:GROUPS]

    for step in range(6):
        for side in range(2):
            x_copy(step, side).wait_send()
            near_copy(step, side, core).wait_send()
    for n in range(9):
        across_copy(n).wait_send()
    for slot in range(1, 8):
        for h in range(2):
            g_copy(slot, h).wait_send()
    for copy in returns:
        copy.wait_send()


def hand_out(bias, scalars, share, bias_out, coulomb_out, exchange_out, weight_out, share_out):
    bias_out[...] = bias[...]
    share_out[...] = share[...]
    for w in range(2):
        coulomb_out[w] = scalars[w]
        exchange_out[w] = scalars[2 + w]
        weight_out[w] = scalars[4 + w]


def local(greens, cholesky, fields, log_weight, group_of):
    f32, bf16 = jnp.float32, jnp.bfloat16
    dma = pltpu.SemaphoreType.DMA
    vmem = pl.BlockSpec(memory_space=pltpu.VMEM)
    smem = pl.BlockSpec(memory_space=pltpu.SMEM)
    hbm = pl.BlockSpec(memory_space=pl.ANY)
    bias, scalars, share = pl.pallas_call(
        kernel,
        out_shape=[
            jax.ShapeDtypeStruct((2, 176), f32),
            jax.ShapeDtypeStruct((6,), f32),
            jax.ShapeDtypeStruct((1, GROUPS), f32),
        ],
        in_specs=[hbm, hbm, vmem, smem, smem],
        out_specs=[vmem, smem, vmem],
        scratch_shapes=[
            pltpu.VMEM((44, 100, 1000), bf16),
            pltpu.VMEM((16, 100, 1000), bf16),
            pltpu.VMEM((BLOCK * ROWS, 256), f32),
            pltpu.VMEM((BLOCK * ROWS, 256), f32),
            pltpu.VMEM((16, 128, 128), f32),
            pltpu.VMEM((16, 8, 128), f32),
            pltpu.VMEM((128, 128), f32),
            pltpu.VMEM((8, 8, 128), f32),
            pltpu.VMEM((8, 8, 128), f32),
            pltpu.VMEM((4, 8, 128), f32),
            pltpu.VMEM((2, 8, 128), f32),
            pltpu.VMEM((2, 16, 8, 128), f32),
            dma((2,)),
            dma((6, 2)),
            dma((6, 2)),
            dma((6, 2)),
            dma((6, 2)),
            dma((9,)),
            dma((9,)),
            dma((9,)),
            dma((8, 2)),
            dma((8, 2)),
            dma((8,)),
            dma((8,)),
            dma((2,)),
            dma((2,)),
        ],
        compiler_params=pltpu.CompilerParams(
            collective_id=0, has_side_effects=True, vmem_limit_bytes=56 * 2**20
        ),
        cost_estimate=pl.CostEstimate(flops=14_080_000_000, bytes_accessed=6_000_000, transcendentals=256),
    )(greens, cholesky, fields, log_weight, group_of)
    pair = jax.ShapeDtypeStruct((2,), f32)
    bias, coulomb, exchange, weight, share = pl.pallas_call(
        hand_out,
        out_shape=[bias, pair, pair, pair, share],
        in_specs=[vmem, smem, vmem],
        out_specs=[vmem, smem, smem, smem, vmem],
    )(bias, scalars, share)
    return bias, coulomb, exchange, weight, share.reshape(GROUPS)


def solution(mesh):
    in_specs = (
        P(("walk", "chol"), None, None, None),
        P("chol", None, None, None),
        P(("walk", "chol"), None),
        P(("walk", "chol")),
        P(("walk", "chol")),
    )
    out_specs = (
        P(("walk", "chol"), None),
        P(("walk", "chol")),
        P(("walk", "chol")),
        P(("walk", "chol")),
        P(),
    )
    return jax.shard_map(local, mesh=mesh, in_specs=in_specs, out_specs=out_specs, check_vma=False)
```

```python
import jax
import jax.numpy as jnp
import numpy as np
from jax import lax
from jax.experimental import pallas as pl
from jax.experimental.pallas import tpu as pltpu
from jax.sharding import PartitionSpec as P

GROUPS = 16
ROWS = 104
STREAM = 8
PLANES = 44
MESH = pl.DeviceIdType.MESH
HIGHEST = lax.Precision.HIGHEST

SLOTS = ((0, 0), (1, 0), (0, -1), (0, 1), (1, -1), (0, 2), (1, 1), (1, -2))
WALKERS = (
    (0, 0), (0, 1), (1, 0), (2, 0), (3, 0), (1, 1), (2, 1), (3, 1),
    (4, 0), (5, 0), (4, 1), (5, 1), (6, 0), (7, 0), (6, 1), (7, 1),
)
QUARTERS = ((0, 1), (3, 6), (5, 7), (2, 4))

STEPS = (
    ((-1, 0), (1, 2)),
    ((-1, 1), (1, 0)),
    ((2, 0), (2, 2)),
    ((-1, 2), (1, 3)),
    ((2, 1), (1, 1)),
    ((-1, 3), (2, 3)),
)
ACROSS = ((0, 0), (0, 1), (1, 0), (1, 1), (2, 0), (2, 1), (3, 0), (4, 0), (4, 1))
FAR_FIRST = (
    (10, 6, 14, 9, 11, 5, 7, 13, 15, 8, 2, 4, 12, 1, 3),
    (8, 7, 9, 6, 10, 5, 11, 4, 12, 3, 13, 2, 14, 1, 15),
)
STEP_PLACE = (11, 15, 23, 27, 34, 40)
ACROSS_PLACE = (19, 20, 21, 22, 31, 32, 33, 38, 39)


def task_list():
    walkers = PLANES

    def early(*pairs):
        return [(walkers, 2 * pair) for pair in pairs]

    def blocks(numbers, *pairs):
        return [(8 * number, walkers + 2 * pair) for pair in pairs for number in numbers]

    tasks = blocks((0,), 0, 1, 2, 3) + early(4, 5, 6, 7, 8)
    tasks += blocks((0, 1), 4) + early(9, 10, 11, 12) + blocks((2,), 4)
    tasks += blocks((0, 1, 2), 5) + early(13, 14)
    tasks += blocks((0, 1, 2), 6) + early(15, 16, 17, 18) + blocks((3,), 4, 5, 6)
    tasks += blocks((0, 1, 2, 3), 7) + early(19, 20, 21) + blocks((4,), 4, 5, 6, 7)
    return tasks + [(walkers + 8, 40), (walkers + 8, 42)]


TASKS = task_list()


def segments(values):
    found, start = [], 0
    while start < len(values):
        end = start + 1
        slope = values[end] - values[start] if end < len(values) else 0
        while end < len(values) and values[end] == values[start] + slope * (end - start):
            end += 1
        found.append((end, start, values[start], slope))
        start = end
    return found


def lookup(values, t):
    result = None
    for end, start, value, slope in reversed(segments(values)):
        here = value + (t - start) * slope if slope else jnp.int32(value)
        result = here if result is None else jnp.where(t < end, here, result)
    return result


def device(x, y, z, core):
    return {"walk": (y * 2 + lax.div(z, 4)) * 2 + core, "chol": lax.rem(z, 4) * 4 + x}


def kernel(
    greens, cholesky, fields, log_weight, group_of,
    bias_out, scalars_out, share_out,
    raw_c, raw_g, others, items, prods_a, prods_b, bias_rows, exch, order,
    back, back_in, combined, stage_out, stage_in,
    local_sem, x_send, x_recv, near_send, near_recv, y_send, y_recv, far_recv,
    g_send, g_recv, b_send, b_recv, s_send, s_recv,
):
    wi, ci = lax.axis_index("walk"), lax.axis_index("chol")
    core = lax.rem(wi, 2)
    y = lax.div(wi, 4)
    z_lo = lax.div(ci, 4)
    z = lax.rem(lax.div(wi, 2), 2) * 4 + z_lo
    x = lax.rem(ci, 4)
    spin = lax.div(y, 2)
    mate = 3 - y
    odd = lax.rem(y, 2)
    neighbour = y + 1 - 2 * odd
    sends_across = core == odd

    def at_x(offset):
        return lax.rem(x + offset + 4, 4)

    def at_z(offset):
        return lax.rem(z + offset + 8, 8)

    def stage_peer(stage, r):
        if stage == 0:
            p = lax.rem(y * 4 + x + r, 16)
            return device(lax.rem(p, 4), lax.div(p, 4), z, core)
        p = lax.rem(z * 2 + core + r, 16)
        return device(x, y, lax.div(p, 2), lax.rem(p, 2))

    own_c = pltpu.make_async_copy(cholesky, raw_c, local_sem.at[0])
    own_g = pltpu.make_async_copy(greens, raw_g, local_sem.at[1])
    own_g.start()
    own_c.start()

    barrier = pltpu.get_barrier_semaphore()

    def greet(peer):
        pl.semaphore_signal(barrier, inc=1, device_id=peer, device_id_type=MESH)

    for stage in range(2):
        def greet_stage(r, _, stage=stage):
            greet(stage_peer(stage, r))
            return 0
        lax.fori_loop(1, 16, greet_stage, 0)
    for offset in (-2, -1, 1, 2):
        greet(device(x, mate, at_z(offset), core))

    def plane_of(i, c):
        first = 3 * odd + 4 * c
        return first + odd + i if i < 3 else first + 3 * (1 - odd)

    def place(step, side, c):
        return STEP_PLACE[step] + side * 2 + c

    lanes = lax.broadcasted_iota(jnp.int32, (1, 128), 1)
    rows = [(i, x * 11 + i) for i in range(11)]
    for step in range(6):
        for side in range(2):
            home, i = STEPS[step][side]
            for c in range(2):
                rows.append((place(step, side, c), at_x(home) * 11 + plane_of(i, c)))
    for n, (step, side) in enumerate(ACROSS):
        home, i = STEPS[step][side]
        rows.append((ACROSS_PLACE[n], at_x(home) * 11 + 8 * (1 - odd) + i))
    rows.append((44, 44))
    def by_spin(pair):
        apart = jnp.swapaxes(pair, 0, 1)
        low = spin == 0
        return jnp.where(low, apart[0], apart[1]), jnp.where(low, apart[1], apart[0])

    own_g.wait()
    for h in range(2):
        items[PLANES + h], others[h] = by_spin(raw_g[h])
    own_c.wait()

    def take(i, _):
        items[i] = by_spin(raw_c[i])[0]
        return 0

    lax.fori_loop(0, 11, take, 0)
    pl.semaphore_wait(barrier, 34)

    sibling = device(x, y, z, 1 - core)
    to_side = (device(at_x(1), y, z, core), device(at_x(-1), y, z, core))

    def x_copy(step, side):
        home, i = STEPS[step][side]
        if home == 2:
            before = STEPS.index(next(s for s in STEPS if s[side] == ((-1, 1)[side], i)))
            src = items.at[place(before, side, core)]
        else:
            src = items.at[plane_of(i, core)]
        return pltpu.make_async_remote_copy(
            src_ref=src, dst_ref=items.at[place(step, side, core)],
            send_sem=x_send.at[step, side], recv_sem=x_recv.at[step, side],
            device_id=to_side[side], device_id_type=MESH,
        )

    def near_copy(step, side, c):
        ref = items.at[place(step, side, c)]
        return pltpu.make_async_remote_copy(
            src_ref=ref, dst_ref=ref, send_sem=near_send.at[step, side], recv_sem=near_recv.at[step, side],
            device_id=sibling, device_id_type=MESH,
        )

    def across_copy(n):
        step, side = ACROSS[n]
        return pltpu.make_async_remote_copy(
            src_ref=items.at[place(step, side, core)], dst_ref=items.at[ACROSS_PLACE[n]],
            send_sem=y_send.at[n], recv_sem=y_recv.at[n],
            device_id=device(x, neighbour, z, core), device_id_type=MESH,
        )

    def onward_copy(n):
        ref = items.at[ACROSS_PLACE[n]]
        return pltpu.make_async_remote_copy(
            src_ref=ref, dst_ref=ref, send_sem=y_send.at[n], recv_sem=far_recv.at[n],
            device_id=sibling, device_id_type=MESH,
        )

    up, down = device(x, y, at_z(1), core), device(x, y, at_z(-1), core)

    def g_copy(slot, h):
        if slot < 4:
            src = others.at[h] if slot == 1 else items.at[PLANES + h]
        else:
            src = items.at[PLANES + WALKERS.index(({4: 1, 5: 3, 6: 1, 7: 4}[slot], h))]
        peer = device(x, mate, z, core) if slot == 1 else up if slot in (2, 4, 7) else down
        return pltpu.make_async_remote_copy(
            src_ref=src, dst_ref=items.at[PLANES + WALKERS.index((slot, h))],
            send_sem=g_send.at[slot, h], recv_sem=g_recv.at[slot, h],
            device_id=peer, device_id_type=MESH,
        )

    def x_start(step):
        for side in range(2):
            x_copy(step, side).start()

    def x_arrived(step):
        for side in range(2):
            x_copy(step, side).wait_recv()
            near_copy(step, side, core).start()

        @pl.when(sends_across)
        def _():
            for n, (s, _side) in enumerate(ACROSS):
                if s == step:
                    across_copy(n).start()

    def across_arrived(numbers):
        @pl.when(jnp.logical_not(sends_across))
        def _():
            for n in numbers:
                across_copy(n).wait_recv()
                onward_copy(n).start()

    def near_arrived(*steps):
        for step in steps:
            for side in range(2):
                near_copy(step, side, 1 - core).wait_recv()

    def onward_arrived(numbers):
        @pl.when(sends_across)
        def _():
            for n in numbers:
                onward_copy(n).wait_recv()

    def begin(step):
        g_copy(1, step).start()
        x_start(step)
        g_copy(2, step).start()
        g_copy(3, step).start()

    begin(0)
    order[...] = jnp.zeros_like(order)
    for at, row in rows:
        order[at : at + 1, :] = (lanes == row).astype(jnp.float32)
    bias_rows[...] = jnp.zeros_like(bias_rows)
    exch[...] = jnp.zeros_like(exch)
    prods_b[...] = jnp.zeros_like(prods_b)
    back[...] = jnp.zeros_like(back)

    row = lax.broadcasted_iota(jnp.int32, (ROWS, 128), 0)
    col = lax.broadcasted_iota(jnp.int32, (ROWS, 128), 1)
    diagonal = row == col
    gap = jnp.zeros((28, 1000), jnp.bfloat16)

    def task(t):
        return lookup([a for a, _ in TASKS], t), lookup([b for _, b in TASKS], t)

    def product(t, buf):
        first, pair = task(t)
        lhs = [part for i in range(STREAM) for part in (items[first + i], gap[: ROWS - 100])]
        rhs = [items[pair], gap, items[pair + 1], gap]
        buf[...] = lax.dot_general(
            jnp.concatenate(lhs, axis=0), jnp.concatenate(rhs, axis=0), (((1,), (1,)), ((), ())),
            preferred_element_type=jnp.float32,
        )

    def reduce(t, buf):
        first, pair = task(t)
        streams_walkers = first >= PLANES
        for h in range(2):
            for g in range(STREAM):
                walker = jnp.where(streams_walkers, first + g, pair + h) - PLANES
                plane = jnp.where(streams_walkers, pair + h, first + g)
                p = buf[g * ROWS : (g + 1) * ROWS, h * 128 : (h + 1) * 128]
                turned = p.T
                q = p[:, :ROWS] * turned[:ROWS, :]
                exch[walker, :, 0:ROWS] += jnp.sum(q.reshape(ROWS // 8, 8, ROWS), axis=0)
                d = jnp.sum(jnp.where(diagonal, p, 0.0).reshape(ROWS // 8, 8, 128), axis=0)
                bias_rows[walker, pl.ds(plane, 1), :] = jnp.sum(d, axis=0, keepdims=True)

    def before(t, parity):
        def at(when, work):
            if when % 2 == parity:
                pl.when(t == when)(work)

        def walker(slot, h, *onward):
            g_copy(slot, h).wait_recv()
            for later in onward:
                g_copy(later, h).start()

        def first(h):
            if h == 0:
                begin(1)
            x_arrived(h)
            x_start(h + 2)
            walker(3, h, 5)
            walker(1, h, 4)
            walker(2, h)

        def second():
            x_arrived(2)
            x_start(4)
            walker(4, 0, 7, 6)
            walker(5, 0)
            across_arrived((0, 1, 2, 3))

        def third():
            near_arrived(2)
            onward_arrived((0, 1, 2, 3))

        def fourth():
            x_arrived(3)
            x_start(5)
            walker(4, 1, 7, 6)
            walker(5, 1)

        def fifth():
            x_arrived(4)
            walker(6, 0)
            walker(7, 0)
            across_arrived((4, 5, 6))

        def sixth():
            near_arrived(4)
            onward_arrived((4, 5, 6))

        def seventh():
            x_arrived(5)
            walker(6, 1)
            walker(7, 1)
            across_arrived((7, 8))

        def eighth():
            near_arrived(5)
            onward_arrived((7, 8))

        at(1, lambda: first(0))
        at(2, lambda: first(1))
        at(5, lambda: near_arrived(0, 1))
        at(9, second)
        at(11, third)
        at(16, fourth)
        at(19, lambda: near_arrived(3))
        at(21, fifth)
        at(24, sixth)
        at(31, seventh)
        at(35, eighth)

    def body(k, _):
        before(2 * k, 0)
        @pl.when(k >= 0)
        def _():
            product(2 * k, prods_a)
            reduce(jnp.maximum(2 * k - 1, 0), prods_b)
        before(2 * k + 1, 1)
        @pl.when(k >= 0)
        def _():
            product(2 * k + 1, prods_b)
            reduce(2 * k, prods_a)
        return 0

    lax.fori_loop(0, len(TASKS) // 2, body, 0)
    reduce(jnp.int32(len(TASKS) - 1), prods_b)

    for w in range(16):
        bias_rows[w, 44:45, :] = jnp.sum(exch[w], axis=0, keepdims=True)
    sums = lax.dot_general(
        jnp.ones((8, 128), jnp.float32), bias_rows[...].reshape(16 * 128, 128), (((1,), (1,)), ((), ())),
        precision=HIGHEST, preferred_element_type=jnp.float32,
    )
    sums = jnp.concatenate([sums[0:1, w * 128 : (w + 1) * 128] for w in range(16)], axis=0)
    sums = jnp.dot(sums, order[...], precision=HIGHEST, preferred_element_type=jnp.float32)
    for slot in range(8):
        for h in range(2):
            w = WALKERS.index((slot, h))
            back[slot, h : h + 1] = sums[w : w + 1]
    returns = []
    for slot, (other, offset) in enumerate(SLOTS):
        if slot:
            copy = pltpu.make_async_remote_copy(
                src_ref=back.at[slot], dst_ref=back_in.at[slot], send_sem=b_send.at[slot], recv_sem=b_recv.at[slot],
                device_id=device(x, mate if other else y, at_z(offset), core), device_id_type=MESH,
            )
            copy.start()
            returns.append(copy)
    for copy in returns:
        copy.wait_recv()
    for quarter, (s, t) in enumerate(QUARTERS):
        combined[quarter] = (back[0] if s == 0 else back_in[s]) + back_in[t]
    lane = lax.broadcasted_iota(jnp.int32, (8, 128), 1)
    bias, exch_sum = None, None
    for m in range(4):
        block = combined[lax.rem(z_lo - m + 4, 4)]
        energy = jnp.sum(jnp.where(lane == 44, block, 0.0), axis=1, keepdims=True)
        wide = jnp.concatenate([jnp.where(lane < 44, block, 0.0), jnp.zeros((8, 128), jnp.float32)], axis=1)
        if m:
            wide = pltpu.roll(wide, 44 * m, 1)
        bias = wide if bias is None else bias + wide
        exch_sum = energy if exch_sum is None else exch_sum + energy
    bias, exch_sum = bias[0:2, 0:176], exch_sum[0:2]
    first = lax.broadcasted_iota(jnp.int32, (2, 1), 0) == 0
    root = np.sqrt(np.float32(176))
    coulomb = jnp.sum(bias * bias, axis=1, keepdims=True) / (2.0 * root)
    exchange = -exch_sum / (2.0 * root)
    importance = jnp.sum(fields[...] * bias - 0.5 * bias * bias, axis=1, keepdims=True) / root
    weight = jnp.where(first, log_weight[0], log_weight[1]) + importance - coulomb - exchange
    member = lax.broadcasted_iota(jnp.int32, (2, 128), 1) == jnp.where(
        lax.broadcasted_iota(jnp.int32, (2, 128), 0) == 0, group_of[0], group_of[1]
    )
    group = jnp.sum(jnp.where(member, jnp.exp(weight), 0.0), axis=0, keepdims=True)

    for stage in range(2):
        me = y * 4 + x if stage == 0 else z * 2 + core
        group = jnp.broadcast_to(group, (8, 128))
        stage_out[stage] = group
        stage_in[stage, 0] = group
        for r in FAR_FIRST[stage]:
            pltpu.make_async_remote_copy(
                src_ref=stage_out.at[stage], dst_ref=stage_in.at[stage, r],
                send_sem=s_send.at[stage], recv_sem=s_recv.at[stage],
                device_id=stage_peer(stage, r), device_id_type=MESH,
            ).start()
        if stage == 0:
            bias_out[...] = bias
            for w in range(2):
                scalars_out[w] = jnp.sum(coulomb[w : w + 1])
                scalars_out[2 + w] = jnp.sum(exchange[w : w + 1])
                scalars_out[4 + w] = jnp.sum(weight[w : w + 1])
        everyone = stage_in.at[stage, pl.ds(1, 15)]
        whole = pltpu.make_async_remote_copy(
            src_ref=everyone, dst_ref=everyone, send_sem=s_send.at[stage], recv_sem=s_recv.at[stage],
            device_id=sibling, device_id_type=MESH,
        )
        whole.wait_recv()
        whole.wait_send()
        group = None
        for a in range(16):
            term = stage_in[stage, lax.rem(me - a + 16, 16), 0:1, :]
            group = term if group is None else group + term
    share_out[...] = (GROUPS * group / jnp.sum(group, axis=1, keepdims=True))[:, 0:GROUPS]

    for step in range(6):
        for side in range(2):
            x_copy(step, side).wait_send()
            near_copy(step, side, core).wait_send()
    for n in range(9):
        across_copy(n).wait_send()
    for slot in range(1, 8):
        for h in range(2):
            g_copy(slot, h).wait_send()
    for copy in returns:
        copy.wait_send()


def hand_out(bias, scalars, share, bias_out, coulomb_out, exchange_out, weight_out, share_out):
    bias_out[...] = bias[...]
    share_out[...] = share[...]
    for w in range(2):
        coulomb_out[w] = scalars[w]
        exchange_out[w] = scalars[2 + w]
        weight_out[w] = scalars[4 + w]


def local(greens, cholesky, fields, log_weight, group_of):
    f32, bf16 = jnp.float32, jnp.bfloat16
    dma = pltpu.SemaphoreType.DMA
    vmem = pl.BlockSpec(memory_space=pltpu.VMEM)
    smem = pl.BlockSpec(memory_space=pltpu.SMEM)
    hbm = pl.BlockSpec(memory_space=pl.ANY)
    bias, scalars, share = pl.pallas_call(
        kernel,
        out_shape=[
            jax.ShapeDtypeStruct((2, 176), f32),
            jax.ShapeDtypeStruct((6,), f32),
            jax.ShapeDtypeStruct((1, GROUPS), f32),
        ],
        in_specs=[hbm, hbm, vmem, smem, smem],
        out_specs=[vmem, smem, vmem],
        scratch_shapes=[
            pltpu.VMEM((11, 100, 2, 1000), bf16),
            pltpu.VMEM((2, 100, 2, 1000), bf16),
            pltpu.VMEM((2, 100, 1000), bf16),
            pltpu.VMEM((PLANES + 16, 100, 1000), bf16),
            pltpu.VMEM((STREAM * ROWS, 256), f32),
            pltpu.VMEM((STREAM * ROWS, 256), f32),
            pltpu.VMEM((16, 128, 128), f32),
            pltpu.VMEM((16, 8, 128), f32),
            pltpu.VMEM((128, 128), f32),
            pltpu.VMEM((8, 8, 128), f32),
            pltpu.VMEM((8, 8, 128), f32),
            pltpu.VMEM((4, 8, 128), f32),
            pltpu.VMEM((2, 8, 128), f32),
            pltpu.VMEM((2, 16, 8, 128), f32),
            dma((2,)),
            dma((6, 2)),
            dma((6, 2)),
            dma((6, 2)),
            dma((6, 2)),
            dma((9,)),
            dma((9,)),
            dma((9,)),
            dma((8, 2)),
            dma((8, 2)),
            dma((8,)),
            dma((8,)),
            dma((2,)),
            dma((2,)),
        ],
        compiler_params=pltpu.CompilerParams(
            collective_id=0, has_side_effects=True, vmem_limit_bytes=56 * 2**20
        ),
        cost_estimate=pl.CostEstimate(flops=14_080_000_000, bytes_accessed=6_000_000, transcendentals=256),
    )(jnp.transpose(greens, (0, 2, 1, 3)), jnp.transpose(cholesky, (0, 2, 1, 3)), fields, log_weight, group_of)
    pair = jax.ShapeDtypeStruct((2,), f32)
    bias, coulomb, exchange, weight, share = pl.pallas_call(
        hand_out,
        out_shape=[bias, pair, pair, pair, share],
        in_specs=[vmem, smem, vmem],
        out_specs=[vmem, smem, smem, smem, vmem],
    )(bias, scalars, share)
    return bias, coulomb, exchange, weight, share.reshape(GROUPS)


def solution(mesh):
    in_specs = (
        P(("walk", "chol"), None, None, None),
        P("chol", None, None, None),
        P(("walk", "chol"), None),
        P(("walk", "chol")),
        P(("walk", "chol")),
    )
    out_specs = (
        P(("walk", "chol"), None),
        P(("walk", "chol")),
        P(("walk", "chol")),
        P(("walk", "chol")),
        P(),
    )
    return jax.shard_map(local, mesh=mesh, in_specs=in_specs, out_specs=out_specs, check_vma=False)
```

```python
import jax
import jax.numpy as jnp
import numpy as np
from jax import lax
from jax.experimental import pallas as pl
from jax.experimental.pallas import tpu as pltpu
from jax.sharding import PartitionSpec as P

GROUPS = 16
ROWS = 104
STREAM = 8
PLANES = 44
MESH = pl.DeviceIdType.MESH
HIGHEST = lax.Precision.HIGHEST

SLOTS = ((0, 0), (1, 0), (0, -1), (0, 1), (1, -1), (0, 2), (1, 1), (1, -2))
WALKERS = (
    (0, 0), (0, 1), (1, 0), (2, 0), (3, 0), (1, 1), (2, 1), (3, 1),
    (4, 0), (5, 0), (4, 1), (5, 1), (6, 0), (7, 0), (6, 1), (7, 1),
)
QUARTERS = ((0, 1), (3, 6), (5, 7), (2, 4))

STEPS = (
    ((-1, 0), (1, 2)),
    ((-1, 1), (1, 0)),
    ((2, 0), (2, 2)),
    ((-1, 2), (1, 3)),
    ((2, 1), (1, 1)),
    ((-1, 3), (2, 3)),
)
ACROSS = ((0, 0), (0, 1), (1, 0), (1, 1), (2, 0), (2, 1), (3, 0), (4, 0), (4, 1))
STAGES = ((4, 4), (8, 2))
STEP_PLACE = (11, 15, 23, 27, 34, 40)
ACROSS_PLACE = (19, 20, 21, 22, 31, 32, 33, 38, 39)


def task_list():
    walkers = PLANES

    def early(*pairs):
        return [(walkers, 2 * pair) for pair in pairs]

    def blocks(numbers, *pairs):
        return [(8 * number, walkers + 2 * pair) for pair in pairs for number in numbers]

    tasks = blocks((0,), 0, 1, 2, 3) + early(4, 5, 6, 7, 8, 9)
    tasks += blocks((0, 1), 4) + early(10, 11, 12) + blocks((2,), 4)
    tasks += blocks((0, 1, 2), 5) + early(13, 14) + blocks((3,), 4)
    tasks += blocks((0, 1, 2), 6) + early(15, 16, 17, 18) + blocks((3,), 5, 6)
    tasks += blocks((0, 1, 2, 3), 7) + early(19, 20, 21) + blocks((4,), 4, 5, 6, 7)
    return tasks + [(walkers + 8, 40), (walkers + 8, 42)]


TASKS = task_list()


def segments(values):
    found, start = [], 0
    while start < len(values):
        end = start + 1
        slope = values[end] - values[start] if end < len(values) else 0
        while end < len(values) and values[end] == values[start] + slope * (end - start):
            end += 1
        found.append((end, start, values[start], slope))
        start = end
    return found


def lookup(values, t):
    result = None
    for end, start, value, slope in reversed(segments(values)):
        here = value + (t - start) * slope if slope else jnp.int32(value)
        result = here if result is None else jnp.where(t < end, here, result)
    return result


def device(x, y, z, core):
    return {"walk": (y * 2 + lax.div(z, 4)) * 2 + core, "chol": lax.rem(z, 4) * 4 + x}


def kernel(
    greens, cholesky, fields, log_weight, group_of,
    bias_out, scalars_out, share_out,
    raw_first, raw_c, raw_g, others, items, prods_a, prods_b, bias_rows, exch, order,
    back, back_in, combined, stage_out, stage_in,
    local_sem, x_send, x_recv, near_send, near_recv, y_send, y_recv, far_recv,
    g_send, g_recv, b_send, b_recv, s_send, s_recv,
):
    wi, ci = lax.axis_index("walk"), lax.axis_index("chol")
    core = lax.rem(wi, 2)
    y = lax.div(wi, 4)
    z_lo = lax.div(ci, 4)
    z = lax.rem(lax.div(wi, 2), 2) * 4 + z_lo
    x = lax.rem(ci, 4)
    spin = lax.div(y, 2)
    mate = 3 - y
    odd = lax.rem(y, 2)
    neighbour = y + 1 - 2 * odd
    sends_across = core == odd

    def at_x(offset):
        return lax.rem(x + offset + 4, 4)

    def at_z(offset):
        return lax.rem(z + offset + 8, 8)

    def stage_peer(stage, a, b):
        if stage == 0:
            return device(xs[a], ys[b], z, core)
        return device(x, y, zs[a], cores[b])

    xs = [at_x(a) for a in range(4)]
    ys = [lax.rem(y + b, 4) for b in range(4)]
    zs = [at_z(a) for a in range(8)]
    cores = [core, 1 - core]

    own_c = pltpu.make_async_copy(cholesky, raw_c, local_sem.at[0])
    own_g = pltpu.make_async_copy(greens, raw_g, local_sem.at[1])
    first_plane = 3 * odd + 4 * core
    first_c = pltpu.make_async_copy(cholesky.at[pl.ds(first_plane, 4)], raw_first, local_sem.at[2])
    own_g.start()
    first_c.start()
    own_c.start()

    barrier = pltpu.get_barrier_semaphore()

    def greet(peer):
        pl.semaphore_signal(barrier, inc=1, device_id=peer, device_id_type=MESH)

    sibling = device(x, y, z, 1 - core)
    to_side = (device(at_x(1), y, z, core), device(at_x(-1), y, z, core))
    up, down = device(x, y, at_z(1), core), device(x, y, at_z(-1), core)
    for peer in (*to_side, up, down, sibling, device(x, neighbour, z, core), device(x, mate, z, core)):
        greet(peer)

    def plane_of(i, c):
        first = 3 * odd + 4 * c
        return first + odd + i if i < 3 else first + 3 * (1 - odd)

    def place(step, side, c):
        return STEP_PLACE[step] + side * 2 + c

    lanes = lax.broadcasted_iota(jnp.int32, (1, 128), 1)
    rows = [(i, x * 11 + i) for i in range(11)]
    for step in range(6):
        for side in range(2):
            home, i = STEPS[step][side]
            for c in range(2):
                rows.append((place(step, side, c), at_x(home) * 11 + plane_of(i, c)))
    for n, (step, side) in enumerate(ACROSS):
        home, i = STEPS[step][side]
        rows.append((ACROSS_PLACE[n], at_x(home) * 11 + 8 * (1 - odd) + i))
    rows.append((44, 44))
    def by_spin(pair):
        apart = jnp.swapaxes(pair, 0, 1)
        low = spin == 0
        return jnp.where(low, apart[0], apart[1]), jnp.where(low, apart[1], apart[0])

    own_g.wait()
    for h in range(2):
        items[PLANES + h], others[h] = by_spin(raw_g[h])
    first_c.wait()
    for i in range(4):
        items[first_plane + i] = by_spin(raw_first[i])[0]
    pl.semaphore_wait(barrier, 7)

    def x_copy(step, side):
        home, i = STEPS[step][side]
        if home == 2:
            before = STEPS.index(next(s for s in STEPS if s[side] == ((-1, 1)[side], i)))
            src = items.at[place(before, side, core)]
        else:
            src = items.at[plane_of(i, core)]
        return pltpu.make_async_remote_copy(
            src_ref=src, dst_ref=items.at[place(step, side, core)],
            send_sem=x_send.at[step, side], recv_sem=x_recv.at[step, side],
            device_id=to_side[side], device_id_type=MESH,
        )

    def near_copy(step, side, c):
        ref = items.at[place(step, side, c)]
        return pltpu.make_async_remote_copy(
            src_ref=ref, dst_ref=ref, send_sem=near_send.at[step, side], recv_sem=near_recv.at[step, side],
            device_id=sibling, device_id_type=MESH,
        )

    def across_copy(n):
        step, side = ACROSS[n]
        return pltpu.make_async_remote_copy(
            src_ref=items.at[place(step, side, core)], dst_ref=items.at[ACROSS_PLACE[n]],
            send_sem=y_send.at[n], recv_sem=y_recv.at[n],
            device_id=device(x, neighbour, z, core), device_id_type=MESH,
        )

    def onward_copy(n):
        ref = items.at[ACROSS_PLACE[n]]
        return pltpu.make_async_remote_copy(
            src_ref=ref, dst_ref=ref, send_sem=y_send.at[n], recv_sem=far_recv.at[n],
            device_id=sibling, device_id_type=MESH,
        )

    def g_copy(slot, h):
        if slot < 4:
            src = others.at[h] if slot == 1 else items.at[PLANES + h]
        else:
            src = items.at[PLANES + WALKERS.index(({4: 1, 5: 3, 6: 1, 7: 4}[slot], h))]
        peer = device(x, mate, z, core) if slot == 1 else up if slot in (2, 4, 7) else down
        return pltpu.make_async_remote_copy(
            src_ref=src, dst_ref=items.at[PLANES + WALKERS.index((slot, h))],
            send_sem=g_send.at[slot, h], recv_sem=g_recv.at[slot, h],
            device_id=peer, device_id_type=MESH,
        )

    def x_start(step):
        for side in range(2):
            x_copy(step, side).start()

    def x_arrived(step):
        for side in range(2):
            x_copy(step, side).wait_recv()
            near_copy(step, side, core).start()

        @pl.when(sends_across)
        def _():
            for n, (s, _side) in enumerate(ACROSS):
                if s == step:
                    across_copy(n).start()

    def across_arrived(numbers):
        @pl.when(jnp.logical_not(sends_across))
        def _():
            for n in numbers:
                across_copy(n).wait_recv()
                onward_copy(n).start()

    def near_arrived(*steps):
        for step in steps:
            for side in range(2):
                near_copy(step, side, 1 - core).wait_recv()

    def onward_arrived(numbers):
        @pl.when(sends_across)
        def _():
            for n in numbers:
                onward_copy(n).wait_recv()

    def begin(step):
        g_copy(1, step).start()
        x_start(step)
        g_copy(2, step).start()
        g_copy(3, step).start()

    begin(0)
    begin(1)
    own_c.wait()

    def take(i, _):
        at = lax.rem(first_plane + 4 + i, 11)
        items[at] = by_spin(raw_c[at])[0]
        return 0

    lax.fori_loop(0, 7, take, 0)
    order[...] = jnp.zeros_like(order)
    for at, row in rows:
        order[at : at + 1, :] = (lanes == row).astype(jnp.float32)
    bias_rows[...] = jnp.zeros_like(bias_rows)
    exch[...] = jnp.zeros_like(exch)
    prods_b[...] = jnp.zeros_like(prods_b)
    back[...] = jnp.zeros_like(back)

    row = lax.broadcasted_iota(jnp.int32, (ROWS, 128), 0)
    col = lax.broadcasted_iota(jnp.int32, (ROWS, 128), 1)
    diagonal = row == col
    gap = jnp.zeros((28, 1000), jnp.bfloat16)

    def task(t):
        return lookup([a for a, _ in TASKS], t), lookup([b for _, b in TASKS], t)

    def product(t, buf):
        first, pair = task(t)
        lhs = [part for i in range(STREAM) for part in (items[first + i], gap[: ROWS - 100])]
        rhs = [items[pair], gap, items[pair + 1], gap]
        buf[...] = lax.dot_general(
            jnp.concatenate(lhs, axis=0), jnp.concatenate(rhs, axis=0), (((1,), (1,)), ((), ())),
            preferred_element_type=jnp.float32,
        )

    def reduce(t, buf):
        first, pair = task(t)
        streams_walkers = first >= PLANES
        for h in range(2):
            for g in range(STREAM):
                walker = jnp.where(streams_walkers, first + g, pair + h) - PLANES
                plane = jnp.where(streams_walkers, pair + h, first + g)
                p = buf[g * ROWS : (g + 1) * ROWS, h * 128 : (h + 1) * 128]
                turned = p.T
                q = p[:, :ROWS] * turned[:ROWS, :]
                exch[walker, :, 0:ROWS] += jnp.sum(q.reshape(ROWS // 8, 8, ROWS), axis=0)
                d = jnp.sum(jnp.where(diagonal, p, 0.0).reshape(ROWS // 8, 8, 128), axis=0)
                bias_rows[walker, pl.ds(plane, 1), :] = jnp.sum(d, axis=0, keepdims=True)

    def before(t):
        def at(when, work):
            pl.when(t == when)(work)

        def walker(slot, h, *onward):
            g_copy(slot, h).wait_recv()
            for later in onward:
                g_copy(later, h).start()

        def first(h):
            x_arrived(h)
            x_start(h + 2)
            walker(3, h, 5)
            walker(1, h, 4)
            walker(2, h)

        def second():
            near_arrived(0, 1)
            across_arrived((0,))

        def third():
            x_arrived(2)
            x_start(4)
            walker(4, 0, 7, 6)
            walker(5, 0)
            across_arrived((1, 2, 3))

        def fourth():
            near_arrived(2)
            onward_arrived((1, 2, 3))

        def fifth():
            x_arrived(3)
            x_start(5)
            walker(4, 1, 7, 6)
            walker(5, 1)
            across_arrived((4,))

        def sixth():
            x_arrived(4)
            walker(6, 0)
            walker(7, 0)
            across_arrived((5, 6))

        def seventh():
            near_arrived(4)
            onward_arrived((5, 6))

        def eighth():
            x_arrived(5)
            walker(6, 1)
            walker(7, 1)
            across_arrived((7, 8))

        def ninth():
            near_arrived(5)
            onward_arrived((7, 8))

        at(0, lambda: first(0))
        at(2, lambda: first(1))
        at(4, second)
        at(8, lambda: onward_arrived((0,)))
        at(10, third)
        at(12, fourth)
        at(16, fifth)
        at(18, lambda: near_arrived(3))
        at(20, lambda: onward_arrived((4,)))
        at(22, sixth)
        at(24, seventh)
        at(30, eighth)
        at(34, ninth)

    def body(k, _):
        before(2 * k)

        @pl.when(k >= 0)
        def _():
            product(2 * k, prods_a)
            reduce(jnp.maximum(2 * k - 1, 0), prods_b)
            product(2 * k + 1, prods_b)
            reduce(2 * k, prods_a)

        return 0

    lax.fori_loop(0, len(TASKS) // 2, body, 0)
    reduce(jnp.int32(len(TASKS) - 1), prods_b)

    for w in range(16):
        bias_rows[w, 44:45, :] = jnp.sum(exch[w], axis=0, keepdims=True)
    sums = lax.dot_general(
        jnp.ones((8, 128), jnp.float32), bias_rows[...].reshape(16 * 128, 128), (((1,), (1,)), ((), ())),
        precision=HIGHEST, preferred_element_type=jnp.float32,
    )
    sums = jnp.concatenate([sums[0:1, w * 128 : (w + 1) * 128] for w in range(16)], axis=0)
    sums = jnp.dot(sums, order[...], precision=HIGHEST, preferred_element_type=jnp.float32)
    for slot in range(8):
        for h in range(2):
            w = WALKERS.index((slot, h))
            back[slot, h : h + 1] = sums[w : w + 1]
    returns = []
    for slot, (other, offset) in enumerate(SLOTS):
        if slot:
            copy = pltpu.make_async_remote_copy(
                src_ref=back.at[slot], dst_ref=back_in.at[slot], send_sem=b_send.at[slot], recv_sem=b_recv.at[slot],
                device_id=device(x, mate if other else y, at_z(offset), core), device_id_type=MESH,
            )
            copy.start()
            returns.append(copy)
    for copy in returns:
        copy.wait_recv()
    for quarter, (s, t) in enumerate(QUARTERS):
        combined[quarter] = (back[0] if s == 0 else back_in[s]) + back_in[t]
    lane = lax.broadcasted_iota(jnp.int32, (8, 128), 1)
    bias, exch_sum = None, None
    for m in range(4):
        block = combined[lax.rem(z_lo - m + 4, 4)]
        energy = jnp.sum(jnp.where(lane == 44, block, 0.0), axis=1, keepdims=True)
        wide = jnp.concatenate([jnp.where(lane < 44, block, 0.0), jnp.zeros((8, 128), jnp.float32)], axis=1)
        if m:
            wide = pltpu.roll(wide, 44 * m, 1)
        bias = wide if bias is None else bias + wide
        exch_sum = energy if exch_sum is None else exch_sum + energy
    bias, exch_sum = bias[0:2, 0:176], exch_sum[0:2]
    first = lax.broadcasted_iota(jnp.int32, (2, 1), 0) == 0
    root = np.sqrt(np.float32(176))
    coulomb = jnp.sum(bias * bias, axis=1, keepdims=True) / (2.0 * root)
    exchange = -exch_sum / (2.0 * root)
    importance = jnp.sum(fields[...] * bias - 0.5 * bias * bias, axis=1, keepdims=True) / root
    weight = jnp.where(first, log_weight[0], log_weight[1]) + importance - coulomb - exchange
    member = lax.broadcasted_iota(jnp.int32, (2, 128), 1) == jnp.where(
        lax.broadcasted_iota(jnp.int32, (2, 128), 0) == 0, group_of[0], group_of[1]
    )
    group = jnp.sum(jnp.where(member, jnp.exp(weight), 0.0), axis=0, keepdims=True)

    for stage in range(2):
        extent, other = STAGES[stage]
        at, beside = (x, y) if stage == 0 else (z, core)
        group = jnp.broadcast_to(group, (8, 128))
        stage_out[stage] = group
        stage_in[stage, 0] = group
        far_first = sorted(
            ((a, b) for a in range(extent) for b in range(other)),
            key=lambda peer: -min(peer[0], extent - peer[0]) - min(peer[1], other - peer[1]),
        )
        for a, b in far_first[:-1]:
            pltpu.make_async_remote_copy(
                src_ref=stage_out.at[stage], dst_ref=stage_in.at[stage, a + extent * b],
                send_sem=s_send.at[stage], recv_sem=s_recv.at[stage],
                device_id=stage_peer(stage, a, b), device_id_type=MESH,
            ).start()
        if stage == 0:
            bias_out[...] = bias
            for w in range(2):
                scalars_out[w] = jnp.sum(coulomb[w : w + 1])
                scalars_out[2 + w] = jnp.sum(exchange[w : w + 1])
                scalars_out[4 + w] = jnp.sum(weight[w : w + 1])
        everyone = stage_in.at[stage, pl.ds(1, 15)]
        whole = pltpu.make_async_remote_copy(
            src_ref=everyone, dst_ref=everyone, send_sem=s_send.at[stage], recv_sem=s_recv.at[stage],
            device_id=sibling, device_id_type=MESH,
        )
        whole.wait_recv()
        whole.wait_send()
        group = None
        steps_a = [lax.rem(at - a + extent, extent) for a in range(extent)]
        steps_b = [lax.rem(beside - b + other, other) * extent for b in range(other)]
        for b in range(other):
            for a in range(extent):
                term = stage_in[stage, steps_a[a] + steps_b[b], 0:1, :]
                group = term if group is None else group + term
    share_out[...] = (GROUPS * group / jnp.sum(group, axis=1, keepdims=True))[:, 0:GROUPS]

    for step in range(6):
        for side in range(2):
            x_copy(step, side).wait_send()
            near_copy(step, side, core).wait_send()
    for n in range(9):
        across_copy(n).wait_send()
    for slot in range(1, 8):
        for h in range(2):
            g_copy(slot, h).wait_send()
    for copy in returns:
        copy.wait_send()


def hand_out(bias, scalars, share, bias_out, coulomb_out, exchange_out, weight_out, share_out):
    bias_out[...] = bias[...]
    share_out[...] = share[...]
    for w in range(2):
        coulomb_out[w] = scalars[w]
        exchange_out[w] = scalars[2 + w]
        weight_out[w] = scalars[4 + w]


def local(greens, cholesky, fields, log_weight, group_of):
    f32, bf16 = jnp.float32, jnp.bfloat16
    dma = pltpu.SemaphoreType.DMA
    vmem = pl.BlockSpec(memory_space=pltpu.VMEM)
    smem = pl.BlockSpec(memory_space=pltpu.SMEM)
    hbm = pl.BlockSpec(memory_space=pl.ANY)
    bias, scalars, share = pl.pallas_call(
        kernel,
        out_shape=[
            jax.ShapeDtypeStruct((2, 176), f32),
            jax.ShapeDtypeStruct((6,), f32),
            jax.ShapeDtypeStruct((1, GROUPS), f32),
        ],
        in_specs=[hbm, hbm, vmem, smem, smem],
        out_specs=[vmem, smem, vmem],
        scratch_shapes=[
            pltpu.VMEM((4, 100, 2, 1000), bf16),
            pltpu.VMEM((11, 100, 2, 1000), bf16),
            pltpu.VMEM((2, 100, 2, 1000), bf16),
            pltpu.VMEM((2, 100, 1000), bf16),
            pltpu.VMEM((PLANES + 16, 100, 1000), bf16),
            pltpu.VMEM((STREAM * ROWS, 256), f32),
            pltpu.VMEM((STREAM * ROWS, 256), f32),
            pltpu.VMEM((16, 128, 128), f32),
            pltpu.VMEM((16, 8, 128), f32),
            pltpu.VMEM((128, 128), f32),
            pltpu.VMEM((8, 8, 128), f32),
            pltpu.VMEM((8, 8, 128), f32),
            pltpu.VMEM((4, 8, 128), f32),
            pltpu.VMEM((2, 8, 128), f32),
            pltpu.VMEM((2, 16, 8, 128), f32),
            dma((3,)),
            dma((6, 2)),
            dma((6, 2)),
            dma((6, 2)),
            dma((6, 2)),
            dma((9,)),
            dma((9,)),
            dma((9,)),
            dma((8, 2)),
            dma((8, 2)),
            dma((8,)),
            dma((8,)),
            dma((2,)),
            dma((2,)),
        ],
        compiler_params=pltpu.CompilerParams(
            collective_id=0, has_side_effects=True, vmem_limit_bytes=56 * 2**20
        ),
        cost_estimate=pl.CostEstimate(flops=14_080_000_000, bytes_accessed=6_000_000, transcendentals=256),
    )(jnp.transpose(greens, (0, 2, 1, 3)), jnp.transpose(cholesky, (0, 2, 1, 3)), fields, log_weight, group_of)
    pair = jax.ShapeDtypeStruct((2,), f32)
    bias, coulomb, exchange, weight, share = pl.pallas_call(
        hand_out,
        out_shape=[bias, pair, pair, pair, share],
        in_specs=[vmem, smem, vmem],
        out_specs=[vmem, smem, smem, smem, vmem],
    )(bias, scalars, share)
    return bias, coulomb, exchange, weight, share.reshape(GROUPS)


def solution(mesh):
    in_specs = (
        P(("walk", "chol"), None, None, None),
        P("chol", None, None, None),
        P(("walk", "chol"), None),
        P(("walk", "chol")),
        P(("walk", "chol")),
    )
    out_specs = (
        P(("walk", "chol"), None),
        P(("walk", "chol")),
        P(("walk", "chol")),
        P(("walk", "chol")),
        P(),
    )
    return jax.shard_map(local, mesh=mesh, in_specs=in_specs, out_specs=out_specs, check_vma=False)
```

```python
import jax
import jax.numpy as jnp
import numpy as np
from jax import lax
from jax.experimental import pallas as pl
from jax.experimental.pallas import tpu as pltpu
from jax.sharding import PartitionSpec as P

GROUPS = 16
ROWS = 104
STREAM = 8
PLANES = 44
MESH = pl.DeviceIdType.MESH
HIGHEST = lax.Precision.HIGHEST

SLOTS = ((0, 0), (1, 0), (0, -1), (0, 1), (1, -1), (0, 2), (1, 1), (1, -2))
WALKERS = (
    (0, 0), (0, 1), (1, 0), (2, 0), (3, 0), (1, 1), (2, 1), (3, 1),
    (4, 0), (5, 0), (4, 1), (5, 1), (6, 0), (7, 0), (6, 1), (7, 1),
)
QUARTERS = ((0, 1), (3, 6), (5, 7), (2, 4))

STEPS = (
    ((-1, 0), (1, 2)),
    ((-1, 1), (1, 0)),
    ((2, 0), (2, 2)),
    ((-1, 2), (1, 3)),
    ((2, 1), (1, 1)),
    ((-1, 3), (2, 3)),
)
ACROSS = ((0, 0), (0, 1), (1, 0), (1, 1), (2, 0), (2, 1), (3, 0), (4, 0), (4, 1))
STAGES = ((4, 4), (8, 2))
STEP_PLACE = (11, 15, 23, 27, 34, 40)
ACROSS_PLACE = (19, 20, 21, 22, 31, 32, 33, 38, 39)


REPEATS = 30


def task_list():
    walkers = PLANES

    def early(*pairs):
        return [(walkers, 2 * pair) for pair in pairs]

    def blocks(numbers, *pairs):
        return [(8 * number, walkers + 2 * pair) for pair in pairs for number in numbers]

    tasks = blocks((0,), 0, 1, 2, 3) + early(4, 5, 6, 7, 8, 9)
    tasks += blocks((0, 1), 4) + early(10, 12, 11) + blocks((2,), 4)
    tasks += blocks((0, 1, 2), 5) + early(13, 14) + blocks((3,), 4, 5) + early(15)
    tasks += blocks((0, 1, 2), 6) + early(16, 17, 18) + blocks((3,), 6)
    tasks += [(REPEATS, walkers + 2 * pair) for pair in (4, 5, 6)]
    tasks += blocks((0, 1, 2, 3), 7) + [(REPEATS, walkers + 14)] + early(20, 21, 19)
    return tasks + [(walkers + 8, 2 * pair) for pair in (20, 21, 19)]


TASKS = task_list()


def segments(values):
    found, start = [], 0
    while start < len(values):
        end = start + 1
        slope = values[end] - values[start] if end < len(values) else 0
        while end < len(values) and values[end] == values[start] + slope * (end - start):
            end += 1
        found.append((end, start, values[start], slope))
        start = end
    return found


def lookup(values, t):
    def pick(found):
        if len(found) == 1:
            _, start, value, slope = found[0]
            return value + (t - start) * slope if slope else jnp.int32(value)
        half = len(found) // 2
        return jnp.where(t < found[half - 1][0], pick(found[:half]), pick(found[half:]))

    return pick(segments(values))


def device(x, y, z, core):
    return {"walk": (y * 2 + lax.div(z, 4)) * 2 + core, "chol": lax.rem(z, 4) * 4 + x}


def kernel(
    greens, cholesky, fields, log_weight, group_of,
    bias_out, scalars_out, share_out,
    raw_first, raw_c, raw_g, others, items, prods_a, prods_b, bias_rows, exch, order,
    back, back_in, combined, stage_out, stage_in,
    local_sem, x_send, x_recv, near_send, near_recv, y_send, y_recv, far_recv,
    g_send, g_recv, b_send, b_recv, s_send, s_recv,
):
    wi, ci = lax.axis_index("walk"), lax.axis_index("chol")
    core = lax.rem(wi, 2)
    y = lax.div(wi, 4)
    z_lo = lax.div(ci, 4)
    z = lax.rem(lax.div(wi, 2), 2) * 4 + z_lo
    x = lax.rem(ci, 4)
    spin = lax.div(y, 2)
    mate = 3 - y
    odd = lax.rem(y, 2)
    neighbour = y + 1 - 2 * odd
    sends_across = core == odd

    def at_x(offset):
        return lax.rem(x + offset + 4, 4)

    def at_z(offset):
        return lax.rem(z + offset + 8, 8)

    def stage_peer(stage, a, b):
        if stage == 0:
            return device(xs[a], ys[b], z, core)
        return device(x, y, zs[a], cores[b])

    xs = [at_x(a) for a in range(4)]
    ys = [lax.rem(y + b, 4) for b in range(4)]
    zs = [at_z(a) for a in range(8)]
    cores = [core, 1 - core]

    own_c = pltpu.make_async_copy(cholesky, raw_c, local_sem.at[0])
    own_g = pltpu.make_async_copy(greens, raw_g, local_sem.at[1])
    first_plane = 3 * odd + 4 * core
    first_c = pltpu.make_async_copy(cholesky.at[pl.ds(first_plane, 4)], raw_first, local_sem.at[2])
    own_g.start()
    first_c.start()
    own_c.start()

    barrier = pltpu.get_barrier_semaphore()

    def greet(peer):
        pl.semaphore_signal(barrier, inc=1, device_id=peer, device_id_type=MESH)

    sibling = device(x, y, z, 1 - core)
    to_side = (device(at_x(1), y, z, core), device(at_x(-1), y, z, core))
    up, down = device(x, y, at_z(1), core), device(x, y, at_z(-1), core)
    for peer in (*to_side, up, down, sibling, device(x, neighbour, z, core), device(x, mate, z, core)):
        greet(peer)

    def plane_of(i, c):
        first = 3 * odd + 4 * c
        return first + odd + i if i < 3 else first + 3 * (1 - odd)

    def place(step, side, c):
        return STEP_PLACE[step] + side * 2 + c

    lanes = lax.broadcasted_iota(jnp.int32, (1, 128), 1)
    rows = [(i, x * 11 + i) for i in range(11)]
    for step in range(6):
        for side in range(2):
            home, i = STEPS[step][side]
            for c in range(2):
                rows.append((place(step, side, c), at_x(home) * 11 + plane_of(i, c)))
    for n, (step, side) in enumerate(ACROSS):
        home, i = STEPS[step][side]
        rows.append((ACROSS_PLACE[n], at_x(home) * 11 + 8 * (1 - odd) + i))
    rows.append((44, 44))
    def by_spin(pair):
        apart = jnp.swapaxes(pair, 0, 1)
        low = spin == 0
        return jnp.where(low, apart[0], apart[1]), jnp.where(low, apart[1], apart[0])

    own_g.wait()
    for h in range(2):
        items[PLANES + h], others[h] = by_spin(raw_g[h])
    first_c.wait()
    for i in range(4):
        items[first_plane + i] = by_spin(raw_first[i])[0]
    pl.semaphore_wait(barrier, 7)

    def x_copy(step, side):
        home, i = STEPS[step][side]
        if home == 2:
            before = STEPS.index(next(s for s in STEPS if s[side] == ((-1, 1)[side], i)))
            src = items.at[place(before, side, core)]
        else:
            src = items.at[plane_of(i, core)]
        return pltpu.make_async_remote_copy(
            src_ref=src, dst_ref=items.at[place(step, side, core)],
            send_sem=x_send.at[step, side], recv_sem=x_recv.at[step, side],
            device_id=to_side[side], device_id_type=MESH,
        )

    def near_copy(step, side, c):
        ref = items.at[place(step, side, c)]
        return pltpu.make_async_remote_copy(
            src_ref=ref, dst_ref=ref, send_sem=near_send.at[step, side], recv_sem=near_recv.at[step, side],
            device_id=sibling, device_id_type=MESH,
        )

    def across_copy(n):
        step, side = ACROSS[n]
        return pltpu.make_async_remote_copy(
            src_ref=items.at[place(step, side, core)], dst_ref=items.at[ACROSS_PLACE[n]],
            send_sem=y_send.at[n], recv_sem=y_recv.at[n],
            device_id=device(x, neighbour, z, core), device_id_type=MESH,
        )

    def onward_copy(n):
        ref = items.at[ACROSS_PLACE[n]]
        return pltpu.make_async_remote_copy(
            src_ref=ref, dst_ref=ref, send_sem=y_send.at[n], recv_sem=far_recv.at[n],
            device_id=sibling, device_id_type=MESH,
        )

    def g_copy(slot, h):
        if slot < 4:
            src = others.at[h] if slot == 1 else items.at[PLANES + h]
        else:
            src = items.at[PLANES + WALKERS.index(({4: 1, 5: 3, 6: 1, 7: 4}[slot], h))]
        peer = device(x, mate, z, core) if slot == 1 else up if slot in (2, 4, 7) else down
        return pltpu.make_async_remote_copy(
            src_ref=src, dst_ref=items.at[PLANES + WALKERS.index((slot, h))],
            send_sem=g_send.at[slot, h], recv_sem=g_recv.at[slot, h],
            device_id=peer, device_id_type=MESH,
        )

    def x_start(step):
        for side in range(2):
            x_copy(step, side).start()

    def x_arrived(step):
        for side in range(2):
            x_copy(step, side).wait_recv()
            near_copy(step, side, core).start()

        @pl.when(sends_across)
        def _():
            for n, (s, _side) in enumerate(ACROSS):
                if s == step:
                    across_copy(n).start()

    def across_arrived(numbers):
        @pl.when(jnp.logical_not(sends_across))
        def _():
            for n in numbers:
                across_copy(n).wait_recv()
                onward_copy(n).start()

    def near_arrived(*steps):
        for step in steps:
            for side in range(2):
                near_copy(step, side, 1 - core).wait_recv()

    def onward_arrived(numbers):
        @pl.when(sends_across)
        def _():
            for n in numbers:
                onward_copy(n).wait_recv()

    def begin(step):
        g_copy(1, step).start()
        x_start(step)
        g_copy(2, step).start()
        g_copy(3, step).start()

    begin(0)
    begin(1)
    own_c.wait()

    def take(i, _):
        at = lax.rem(first_plane + 4 + i, 11)
        items[at] = by_spin(raw_c[at])[0]
        return 0

    lax.fori_loop(0, 7, take, 0)
    order[...] = jnp.zeros_like(order)
    for at, row in rows:
        order[at : at + 1, :] = (lanes == row).astype(jnp.float32)
    bias_rows[...] = jnp.zeros_like(bias_rows)
    exch[...] = jnp.zeros_like(exch)
    prods_b[...] = jnp.zeros_like(prods_b)
    back[...] = jnp.zeros_like(back)

    row = lax.broadcasted_iota(jnp.int32, (ROWS, 128), 0)
    col = lax.broadcasted_iota(jnp.int32, (ROWS, 128), 1)
    diagonal = row == col
    gap = jnp.zeros((28, 1000), jnp.bfloat16)

    def task(t):
        return lookup([a for a, _ in TASKS], t), lookup([b for _, b in TASKS], t)

    def product(t, buf):
        first, pair = task(t)
        lhs = [part for i in range(STREAM) for part in (items[first + i], gap[: ROWS - 100])]
        rhs = [items[pair], gap, items[pair + 1], gap]
        buf[...] = lax.dot_general(
            jnp.concatenate(lhs, axis=0), jnp.concatenate(rhs, axis=0), (((1,), (1,)), ((), ())),
            preferred_element_type=jnp.float32,
        )

    def reduce(t, buf):
        first, pair = task(t)
        streams_walkers = first >= PLANES
        for h in range(2):
            for g in range(STREAM):
                walker = jnp.where(streams_walkers, first + g, pair + h) - PLANES
                plane = jnp.where(streams_walkers, pair + h, first + g)
                p = buf[g * ROWS : (g + 1) * ROWS, h * 128 : (h + 1) * 128]
                turned = p.T
                q = p[:, :ROWS] * turned[:ROWS, :]
                part = jnp.sum(q.reshape(ROWS // 8, 8, ROWS), axis=0)
                if g < 2:
                    part = jnp.where(first == REPEATS, 0.0, part)
                exch[walker, :, 0:ROWS] += part
                d = jnp.sum(jnp.where(diagonal, p, 0.0).reshape(ROWS // 8, 8, 128), axis=0)
                bias_rows[walker, pl.ds(plane, 1), :] = jnp.sum(d, axis=0, keepdims=True)

    def before(t):
        def at(when, work):
            pl.when(t == when)(work)

        def walker(slot, h, *onward):
            g_copy(slot, h).wait_recv()
            for later in onward:
                g_copy(later, h).start()

        def first(h):
            x_arrived(h)
            x_start(h + 2)
            walker(3, h, 5)
            walker(1, h, 4)
            walker(2, h)

        def second():
            near_arrived(0, 1)
            across_arrived((0,))

        def third():
            x_arrived(2)
            x_start(4)
            walker(4, 0, 7, 6)
            walker(5, 0)
            across_arrived((1, 2))

        def fourth():
            near_arrived(2)
            onward_arrived((1, 2))
            across_arrived((3,))

        def fifth():
            x_arrived(3)
            x_start(5)
            walker(4, 1, 7, 6)
            walker(5, 1)
            across_arrived((4,))

        def sixth():
            x_arrived(4)
            walker(6, 0)
            walker(7, 0)
            across_arrived((5, 6))

        def seventh():
            near_arrived(4)
            onward_arrived((5, 6))

        def eighth():
            x_arrived(5)
            walker(6, 1)
            walker(7, 1)

        @pl.when(t < 10)
        def _():
            at(0, lambda: first(0))
            at(2, lambda: first(1))
            at(4, second)
            at(8, lambda: onward_arrived((0,)))

        @pl.when(jnp.logical_and(t >= 10, t < 20))
        def _():
            at(10, third)
            at(12, fourth)
            at(14, lambda: onward_arrived((3,)))
            at(16, fifth)
            at(18, lambda: near_arrived(3))

        @pl.when(jnp.logical_and(t >= 20, t < 28))
        def _():
            at(20, lambda: onward_arrived((4,)))
            at(24, sixth)
            at(26, seventh)

        @pl.when(t >= 34)
        def _():
            at(34, eighth)
            at(36, lambda: across_arrived((7, 8)))
            at(38, lambda: near_arrived(5))
            at(40, lambda: onward_arrived((7, 8)))

    def body(k, _):
        before(2 * k)

        @pl.when(k >= 0)
        def _():
            product(2 * k, prods_a)
            reduce(jnp.maximum(2 * k - 1, 0), prods_b)
            product(2 * k + 1, prods_b)
            reduce(2 * k, prods_a)

        return 0

    lax.fori_loop(0, len(TASKS) // 2, body, 0)
    product(jnp.int32(len(TASKS) - 1), prods_a)
    reduce(jnp.int32(len(TASKS) - 2), prods_b)
    reduce(jnp.int32(len(TASKS) - 1), prods_a)

    for w in range(16):
        bias_rows[w, 44:45, :] = jnp.sum(exch[w], axis=0, keepdims=True)
    wide = jnp.dot(
        bias_rows[...].reshape(16 * 48, 128), jnp.ones((128, 128), jnp.float32),
        precision=HIGHEST, preferred_element_type=jnp.float32,
    ).reshape(16, 48, 128)
    sums = [jnp.sum(wide[w] * order[...], axis=0, keepdims=True) for w in range(16)]
    for slot in range(8):
        for h in range(2):
            back[slot, h : h + 1] = sums[WALKERS.index((slot, h))]
    returns = []
    for slot, (other, offset) in reversed(tuple(enumerate(SLOTS))):
        if slot:
            copy = pltpu.make_async_remote_copy(
                src_ref=back.at[slot], dst_ref=back_in.at[slot], send_sem=b_send.at[slot], recv_sem=b_recv.at[slot],
                device_id=device(x, mate if other else y, at_z(offset), core), device_id_type=MESH,
            )
            copy.start()
            returns.append(copy)
    for copy in returns:
        copy.wait_recv()
    for quarter, (s, t) in enumerate(QUARTERS):
        combined[quarter] = (back[0] if s == 0 else back_in[s]) + back_in[t]
    lane = lax.broadcasted_iota(jnp.int32, (8, 128), 1)
    bias, exch_sum = None, None
    for m in range(4):
        block = combined[lax.rem(z_lo - m + 4, 4)]
        energy = jnp.sum(jnp.where(lane == 44, block, 0.0), axis=1, keepdims=True)
        wide = jnp.concatenate([jnp.where(lane < 44, block, 0.0), jnp.zeros((8, 128), jnp.float32)], axis=1)
        if m:
            wide = pltpu.roll(wide, 44 * m, 1)
        bias = wide if bias is None else bias + wide
        exch_sum = energy if exch_sum is None else exch_sum + energy
    bias, exch_sum = bias[0:2, 0:176], exch_sum[0:2]
    first = lax.broadcasted_iota(jnp.int32, (2, 1), 0) == 0
    root = np.sqrt(np.float32(176))
    coulomb = jnp.sum(bias * bias, axis=1, keepdims=True) / (2.0 * root)
    exchange = -exch_sum / (2.0 * root)
    importance = jnp.sum(fields[...] * bias - 0.5 * bias * bias, axis=1, keepdims=True) / root
    weight = jnp.where(first, log_weight[0], log_weight[1]) + importance - coulomb - exchange
    member = lax.broadcasted_iota(jnp.int32, (2, 128), 1) == jnp.where(
        lax.broadcasted_iota(jnp.int32, (2, 128), 0) == 0, group_of[0], group_of[1]
    )
    group = jnp.sum(jnp.where(member, jnp.exp(weight), 0.0), axis=0, keepdims=True)

    for stage in range(2):
        extent, other = STAGES[stage]
        at, beside = (x, y) if stage == 0 else (z, core)
        group = jnp.broadcast_to(group, (8, 128))
        stage_out[stage] = group
        stage_in[stage, 0] = group
        far_first = sorted(
            ((a, b) for a in range(extent) for b in range(other)),
            key=lambda peer: -min(peer[0], extent - peer[0]) - min(peer[1], other - peer[1]),
        )
        for a, b in far_first[:-1]:
            pltpu.make_async_remote_copy(
                src_ref=stage_out.at[stage], dst_ref=stage_in.at[stage, a + extent * b],
                send_sem=s_send.at[stage], recv_sem=s_recv.at[stage],
                device_id=stage_peer(stage, a, b), device_id_type=MESH,
            ).start()
        if stage == 0:
            bias_out[...] = bias
            for w in range(2):
                scalars_out[w] = jnp.sum(coulomb[w : w + 1])
                scalars_out[2 + w] = jnp.sum(exchange[w : w + 1])
                scalars_out[4 + w] = jnp.sum(weight[w : w + 1])
        everyone = stage_in.at[stage, pl.ds(1, 15)]
        whole = pltpu.make_async_remote_copy(
            src_ref=everyone, dst_ref=everyone, send_sem=s_send.at[stage], recv_sem=s_recv.at[stage],
            device_id=sibling, device_id_type=MESH,
        )
        whole.wait_recv()
        whole.wait_send()
        group = None
        steps_a = [lax.rem(at - a + extent, extent) for a in range(extent)]
        steps_b = [lax.rem(beside - b + other, other) * extent for b in range(other)]
        for b in range(other):
            for a in range(extent):
                term = stage_in[stage, steps_a[a] + steps_b[b], 0:1, :]
                group = term if group is None else group + term
    share_out[...] = (GROUPS * group / jnp.sum(group, axis=1, keepdims=True))[:, 0:GROUPS]

    for step in range(6):
        for side in range(2):
            x_copy(step, side).wait_send()
            near_copy(step, side, core).wait_send()
    for n in range(9):
        across_copy(n).wait_send()
    for slot in range(1, 8):
        for h in range(2):
            g_copy(slot, h).wait_send()
    for copy in returns:
        copy.wait_send()


def hand_out(bias, scalars, share, bias_out, coulomb_out, exchange_out, weight_out, share_out):
    bias_out[...] = bias[...]
    share_out[...] = share[...]
    for w in range(2):
        coulomb_out[w] = scalars[w]
        exchange_out[w] = scalars[2 + w]
        weight_out[w] = scalars[4 + w]


def local(greens, cholesky, fields, log_weight, group_of):
    f32, bf16 = jnp.float32, jnp.bfloat16
    dma = pltpu.SemaphoreType.DMA
    vmem = pl.BlockSpec(memory_space=pltpu.VMEM)
    smem = pl.BlockSpec(memory_space=pltpu.SMEM)
    hbm = pl.BlockSpec(memory_space=pl.ANY)
    bias, scalars, share = pl.pallas_call(
        kernel,
        out_shape=[
            jax.ShapeDtypeStruct((2, 176), f32),
            jax.ShapeDtypeStruct((6,), f32),
            jax.ShapeDtypeStruct((1, GROUPS), f32),
        ],
        in_specs=[hbm, hbm, vmem, smem, smem],
        out_specs=[vmem, smem, vmem],
        scratch_shapes=[
            pltpu.VMEM((4, 100, 2, 1000), bf16),
            pltpu.VMEM((11, 100, 2, 1000), bf16),
            pltpu.VMEM((2, 100, 2, 1000), bf16),
            pltpu.VMEM((2, 100, 1000), bf16),
            pltpu.VMEM((PLANES + 16, 100, 1000), bf16),
            pltpu.VMEM((STREAM * ROWS, 256), f32),
            pltpu.VMEM((STREAM * ROWS, 256), f32),
            pltpu.VMEM((16, 48, 128), f32),
            pltpu.VMEM((16, 8, 128), f32),
            pltpu.VMEM((48, 128), f32),
            pltpu.VMEM((8, 8, 128), f32),
            pltpu.VMEM((8, 8, 128), f32),
            pltpu.VMEM((4, 8, 128), f32),
            pltpu.VMEM((2, 8, 128), f32),
            pltpu.VMEM((2, 16, 8, 128), f32),
            dma((3,)),
            dma((6, 2)),
            dma((6, 2)),
            dma((6, 2)),
            dma((6, 2)),
            dma((9,)),
            dma((9,)),
            dma((9,)),
            dma((8, 2)),
            dma((8, 2)),
            dma((8,)),
            dma((8,)),
            dma((2,)),
            dma((2,)),
        ],
        compiler_params=pltpu.CompilerParams(
            collective_id=0, has_side_effects=True, vmem_limit_bytes=56 * 2**20
        ),
        cost_estimate=pl.CostEstimate(flops=14_080_000_000, bytes_accessed=6_000_000, transcendentals=256),
    )(jnp.transpose(greens, (0, 2, 1, 3)), jnp.transpose(cholesky, (0, 2, 1, 3)), fields, log_weight, group_of)
    pair = jax.ShapeDtypeStruct((2,), f32)
    bias, coulomb, exchange, weight, share = pl.pallas_call(
        hand_out,
        out_shape=[bias, pair, pair, pair, share],
        in_specs=[vmem, smem, vmem],
        out_specs=[vmem, smem, smem, smem, vmem],
    )(bias, scalars, share)
    return bias, coulomb, exchange, weight, share.reshape(GROUPS)


def solution(mesh):
    in_specs = (
        P(("walk", "chol"), None, None, None),
        P("chol", None, None, None),
        P(("walk", "chol"), None),
        P(("walk", "chol")),
        P(("walk", "chol")),
    )
    out_specs = (
        P(("walk", "chol"), None),
        P(("walk", "chol")),
        P(("walk", "chol")),
        P(("walk", "chol")),
        P(),
    )
    return jax.shard_map(local, mesh=mesh, in_specs=in_specs, out_specs=out_specs, check_vma=False)
```

```python
import jax
import jax.numpy as jnp
import numpy as np
from jax import lax
from jax.experimental import pallas as pl
from jax.experimental.pallas import tpu as pltpu
from jax.sharding import PartitionSpec as P

GROUPS = 16
ROWS = 104
STREAM = 8
PLANES = 44
MESH = pl.DeviceIdType.MESH
HIGHEST = lax.Precision.HIGHEST

SLOTS = ((0, 0), (1, 0), (0, -1), (0, 1), (1, -1), (0, 2), (1, 1), (1, -2))
WALKERS = (
    (0, 0), (0, 1), (1, 0), (2, 0), (3, 0), (1, 1), (2, 1), (3, 1),
    (4, 0), (5, 0), (4, 1), (5, 1), (6, 0), (7, 0), (6, 1), (7, 1),
)
QUARTERS = ((0, 1), (3, 6), (5, 7), (2, 4))

STEPS = (
    ((-1, 0), (1, 2)),
    ((-1, 1), (1, 0)),
    ((2, 0), (2, 2)),
    ((-1, 2), (1, 3)),
    ((2, 1), (1, 1)),
    ((-1, 3), (2, 3)),
)
ACROSS = ((0, 0), (0, 1), (1, 0), (1, 1), (2, 0), (2, 1), (3, 0), (4, 0), (4, 1))
STAGES = ((4, 4), (8, 2))
STEP_PLACE = (11, 15, 23, 27, 34, 40)
ACROSS_PLACE = (19, 20, 21, 22, 31, 32, 33, 38, 39)


REPEATS = 30


def task_list():
    walkers = PLANES

    def early(*pairs):
        return [(walkers, 2 * pair) for pair in pairs]

    def blocks(numbers, *pairs):
        return [(8 * number, walkers + 2 * pair) for pair in pairs for number in numbers]

    tasks = blocks((0,), 0, 1, 2, 3) + early(4, 5, 6, 7, 8, 9)
    tasks += blocks((0, 1), 4) + early(10, 12, 11) + blocks((2,), 4)
    tasks += blocks((0, 1, 2), 5) + early(13, 14) + blocks((3,), 4, 5) + early(15)
    tasks += blocks((0, 1, 2), 6) + early(16, 17, 18) + blocks((3,), 6)
    tasks += [(REPEATS, walkers + 2 * pair) for pair in (4, 5, 6)]
    tasks += blocks((0, 1, 2, 3), 7) + [(REPEATS, walkers + 14)] + early(20, 21, 19)
    return tasks + [(walkers + 8, 2 * pair) for pair in (20, 21, 19)]


TASKS = task_list()


def segments(values):
    found, start = [], 0
    while start < len(values):
        end = start + 1
        slope = values[end] - values[start] if end < len(values) else 0
        while end < len(values) and values[end] == values[start] + slope * (end - start):
            end += 1
        found.append((end, start, values[start], slope))
        start = end
    return found


def lookup(values, t):
    def pick(found):
        if len(found) == 1:
            _, start, value, slope = found[0]
            return value + (t - start) * slope if slope else jnp.int32(value)
        half = len(found) // 2
        return jnp.where(t < found[half - 1][0], pick(found[:half]), pick(found[half:]))

    return pick(segments(values))


def device(x, y, z, core):
    return {"walk": (y * 2 + lax.div(z, 4)) * 2 + core, "chol": lax.rem(z, 4) * 4 + x}


def kernel(
    greens, cholesky, fields, log_weight, group_of,
    bias_out, scalars_out, share_out,
    raw_first, raw_c, raw_g, others, items, prods_a, prods_b, bias_rows, exch, order,
    back, back_in, combined, stage_out, stage_in,
    local_sem, x_send, x_recv, near_send, near_recv, y_send, y_recv, far_recv,
    g_send, g_recv, b_send, b_recv, s_send, s_recv,
):
    wi, ci = lax.axis_index("walk"), lax.axis_index("chol")
    core = lax.rem(wi, 2)
    y = lax.div(wi, 4)
    z_lo = lax.div(ci, 4)
    z = lax.rem(lax.div(wi, 2), 2) * 4 + z_lo
    x = lax.rem(ci, 4)
    spin = lax.div(y, 2)
    mate = 3 - y
    odd = lax.rem(y, 2)
    neighbour = y + 1 - 2 * odd
    sends_across = core == odd

    def at_x(offset):
        return lax.rem(x + offset + 4, 4)

    def at_z(offset):
        return lax.rem(z + offset + 8, 8)

    def stage_peer(stage, a, b):
        if stage == 0:
            return device(xs[a], ys[b], z, core)
        return device(x, y, zs[a], cores[b])

    xs = [at_x(a) for a in range(4)]
    ys = [lax.rem(y + b, 4) for b in range(4)]
    zs = [at_z(a) for a in range(8)]
    cores = [core, 1 - core]

    own_c = pltpu.make_async_copy(cholesky, raw_c, local_sem.at[0])
    own_g = pltpu.make_async_copy(greens, raw_g, local_sem.at[1])
    first_plane = 3 * odd + 4 * core
    first_c = pltpu.make_async_copy(cholesky.at[pl.ds(first_plane, 4)], raw_first, local_sem.at[2])
    own_g.start()
    first_c.start()
    own_c.start()

    barrier = pltpu.get_barrier_semaphore()

    def greet(peer):
        pl.semaphore_signal(barrier, inc=1, device_id=peer, device_id_type=MESH)

    sibling = device(x, y, z, 1 - core)
    to_side = (device(at_x(1), y, z, core), device(at_x(-1), y, z, core))
    up, down = device(x, y, at_z(1), core), device(x, y, at_z(-1), core)
    for peer in (*to_side, up, down, sibling, device(x, neighbour, z, core), device(x, mate, z, core)):
        greet(peer)

    def plane_of(i, c):
        first = 3 * odd + 4 * c
        return first + odd + i if i < 3 else first + 3 * (1 - odd)

    def place(step, side, c):
        return STEP_PLACE[step] + side * 2 + c

    lanes = lax.broadcasted_iota(jnp.int32, (1, 128), 1)
    rows = [(i, x * 11 + i) for i in range(11)]
    for step in range(6):
        for side in range(2):
            home, i = STEPS[step][side]
            for c in range(2):
                rows.append((place(step, side, c), at_x(home) * 11 + plane_of(i, c)))
    for n, (step, side) in enumerate(ACROSS):
        home, i = STEPS[step][side]
        rows.append((ACROSS_PLACE[n], at_x(home) * 11 + 8 * (1 - odd) + i))
    rows.append((44, 44))
    def by_spin(pair):
        apart = jnp.swapaxes(pair, 0, 1)
        low = spin == 0
        return jnp.where(low, apart[0], apart[1]), jnp.where(low, apart[1], apart[0])

    own_g.wait()
    for h in range(2):
        items[PLANES + h], others[h] = by_spin(raw_g[h])
    first_c.wait()
    for i in range(4):
        items[first_plane + i] = by_spin(raw_first[i])[0]
    pl.semaphore_wait(barrier, 7)

    def x_copy(step, side):
        home, i = STEPS[step][side]
        if home == 2:
            before = STEPS.index(next(s for s in STEPS if s[side] == ((-1, 1)[side], i)))
            src = items.at[place(before, side, core)]
        else:
            src = items.at[plane_of(i, core)]
        return pltpu.make_async_remote_copy(
            src_ref=src, dst_ref=items.at[place(step, side, core)],
            send_sem=x_send.at[step, side], recv_sem=x_recv.at[step, side],
            device_id=to_side[side], device_id_type=MESH,
        )

    def near_copy(step, side, c):
        ref = items.at[place(step, side, c)]
        return pltpu.make_async_remote_copy(
            src_ref=ref, dst_ref=ref, send_sem=near_send.at[step, side], recv_sem=near_recv.at[step, side],
            device_id=sibling, device_id_type=MESH,
        )

    def across_copy(n):
        step, side = ACROSS[n]
        return pltpu.make_async_remote_copy(
            src_ref=items.at[place(step, side, core)], dst_ref=items.at[ACROSS_PLACE[n]],
            send_sem=y_send.at[n], recv_sem=y_recv.at[n],
            device_id=device(x, neighbour, z, core), device_id_type=MESH,
        )

    def onward_copy(n):
        ref = items.at[ACROSS_PLACE[n]]
        return pltpu.make_async_remote_copy(
            src_ref=ref, dst_ref=ref, send_sem=y_send.at[n], recv_sem=far_recv.at[n],
            device_id=sibling, device_id_type=MESH,
        )

    def g_copy(slot, h):
        if slot < 4:
            src = others.at[h] if slot == 1 else items.at[PLANES + h]
        else:
            src = items.at[PLANES + WALKERS.index(({4: 1, 5: 3, 6: 1, 7: 4}[slot], h))]
        peer = device(x, mate, z, core) if slot == 1 else up if slot in (2, 4, 7) else down
        return pltpu.make_async_remote_copy(
            src_ref=src, dst_ref=items.at[PLANES + WALKERS.index((slot, h))],
            send_sem=g_send.at[slot, h], recv_sem=g_recv.at[slot, h],
            device_id=peer, device_id_type=MESH,
        )

    def x_start(step):
        for side in range(2):
            x_copy(step, side).start()

    def x_arrived(step):
        for side in range(2):
            x_copy(step, side).wait_recv()
            near_copy(step, side, core).start()

        @pl.when(sends_across)
        def _():
            for n, (s, _side) in enumerate(ACROSS):
                if s == step:
                    across_copy(n).start()

    def across_arrived(numbers):
        @pl.when(jnp.logical_not(sends_across))
        def _():
            for n in numbers:
                across_copy(n).wait_recv()
                onward_copy(n).start()

    def near_arrived(*steps):
        for step in steps:
            for side in range(2):
                near_copy(step, side, 1 - core).wait_recv()

    def onward_arrived(numbers):
        @pl.when(sends_across)
        def _():
            for n in numbers:
                onward_copy(n).wait_recv()

    def begin(step):
        g_copy(1, step).start()
        x_start(step)
        g_copy(2, step).start()
        g_copy(3, step).start()

    begin(0)
    begin(1)
    own_c.wait()

    def take(i, _):
        at = lax.rem(first_plane + 4 + i, 11)
        items[at] = by_spin(raw_c[at])[0]
        return 0

    lax.fori_loop(0, 7, take, 0)
    order[...] = jnp.zeros_like(order)
    for at, row in rows:
        order[at : at + 1, :] = (lanes == row).astype(jnp.float32)
    bias_rows[...] = jnp.zeros_like(bias_rows)
    exch[...] = jnp.zeros_like(exch)
    prods_b[...] = jnp.zeros_like(prods_b)
    back[...] = jnp.zeros_like(back)

    row = lax.broadcasted_iota(jnp.int32, (ROWS, 128), 0)
    col = lax.broadcasted_iota(jnp.int32, (ROWS, 128), 1)
    diagonal = row == col
    gap = jnp.zeros((28, 1000), jnp.bfloat16)

    def task(t):
        return lookup([a for a, _ in TASKS], t), lookup([b for _, b in TASKS], t)

    def product(t, buf):
        first, pair = task(t)
        lhs = [part for i in range(STREAM) for part in (items[first + i], gap[: ROWS - 100])]
        rhs = [items[pair], gap, items[pair + 1], gap]
        buf[...] = lax.dot_general(
            jnp.concatenate(lhs, axis=0), jnp.concatenate(rhs, axis=0), (((1,), (1,)), ((), ())),
            preferred_element_type=jnp.float32,
        )

    def reduce(t, buf):
        first, pair = task(t)
        streams_walkers = first >= PLANES
        for h in range(2):
            for g in range(STREAM):
                walker = jnp.where(streams_walkers, first + g, pair + h) - PLANES
                plane = jnp.where(streams_walkers, pair + h, first + g)
                p = buf[g * ROWS : (g + 1) * ROWS, h * 128 : (h + 1) * 128]
                turned = p.T
                q = p[:, :ROWS] * turned[:ROWS, :]
                part = jnp.sum(q.reshape(ROWS // 8, 8, ROWS), axis=0)
                if g < 2:
                    part = jnp.where(first == REPEATS, 0.0, part)
                exch[walker, :, 0:ROWS] += part
                d = jnp.sum(jnp.where(diagonal, p, 0.0).reshape(ROWS // 8, 8, 128), axis=0)
                bias_rows[walker, pl.ds(plane, 1), :] = jnp.sum(d, axis=0, keepdims=True)

    def before(t):
        def at(when, work):
            pl.when(t == when)(work)

        def walker(slot, h, *onward):
            g_copy(slot, h).wait_recv()
            for later in onward:
                g_copy(later, h).start()

        def first(h):
            x_arrived(h)
            x_start(h + 2)
            walker(3, h, 5)
            walker(1, h, 4)
            walker(2, h)

        def second():
            near_arrived(0, 1)
            across_arrived((0,))

        def third():
            x_arrived(2)
            x_start(4)
            walker(4, 0, 7, 6)
            walker(5, 0)
            across_arrived((1, 2))

        def fourth():
            near_arrived(2)
            onward_arrived((1, 2))
            across_arrived((3,))

        def fifth():
            x_arrived(3)
            x_start(5)
            walker(4, 1, 7, 6)
            walker(5, 1)
            across_arrived((4,))

        def sixth():
            x_arrived(4)
            walker(6, 0)
            walker(7, 0)
            across_arrived((5, 6))

        def seventh():
            near_arrived(4)
            onward_arrived((5, 6))

        def eighth():
            x_arrived(5)
            walker(6, 1)
            walker(7, 1)

        def split(when, early, late):
            lax.cond(t < when, early, late)

        def run(*work):
            def go():
                for when, what in work:
                    at(when, what)
            return go

        split(
            16,
            lambda: split(
                6,
                run((0, lambda: first(0)), (2, lambda: first(1)), (4, second)),
                lambda: split(
                    12,
                    run((8, lambda: onward_arrived((0,))), (10, third)),
                    run((12, fourth), (14, lambda: onward_arrived((3,)))),
                ),
            ),
            lambda: split(
                28,
                lambda: split(
                    22,
                    run((16, fifth), (18, lambda: near_arrived(3)), (20, lambda: onward_arrived((4,)))),
                    run((24, sixth), (26, seventh)),
                ),
                lambda: split(
                    38,
                    run((34, eighth), (36, lambda: across_arrived((7, 8)))),
                    run((38, lambda: near_arrived(5)), (40, lambda: onward_arrived((7, 8)))),
                ),
            ),
        )

    def body(k, _):
        before(2 * k)

        product(2 * k, prods_a)
        reduce(jnp.maximum(2 * k - 1, 0), prods_b)
        product(2 * k + 1, prods_b)
        reduce(2 * k, prods_a)

        return 0

    lax.fori_loop(0, len(TASKS) // 2, body, 0)
    product(jnp.int32(len(TASKS) - 1), prods_a)
    reduce(jnp.int32(len(TASKS) - 2), prods_b)
    reduce(jnp.int32(len(TASKS) - 1), prods_a)

    for w in range(16):
        bias_rows[w, 44:45, :] = jnp.sum(exch[w], axis=0, keepdims=True)
    wide = jnp.dot(
        bias_rows[...].reshape(16 * 48, 128), jnp.ones((128, 128), jnp.float32),
        precision=HIGHEST, preferred_element_type=jnp.float32,
    ).reshape(16, 48, 128)
    sums = [jnp.sum(wide[w] * order[...], axis=0, keepdims=True) for w in range(16)]
    for slot in range(8):
        for h in range(2):
            back[slot, h : h + 1] = sums[WALKERS.index((slot, h))]
    returns = []
    for slot, (other, offset) in reversed(tuple(enumerate(SLOTS))):
        if slot:
            copy = pltpu.make_async_remote_copy(
                src_ref=back.at[slot], dst_ref=back_in.at[slot], send_sem=b_send.at[slot], recv_sem=b_recv.at[slot],
                device_id=device(x, mate if other else y, at_z(offset), core), device_id_type=MESH,
            )
            copy.start()
            returns.append(copy)
    for copy in returns:
        copy.wait_recv()
    for quarter, (s, t) in enumerate(QUARTERS):
        combined[quarter] = (back[0] if s == 0 else back_in[s]) + back_in[t]
    lane = lax.broadcasted_iota(jnp.int32, (8, 128), 1)
    bias, exch_sum = None, None
    for m in range(4):
        block = combined[lax.rem(z_lo - m + 4, 4)]
        energy = jnp.sum(jnp.where(lane == 44, block, 0.0), axis=1, keepdims=True)
        wide = jnp.concatenate([jnp.where(lane < 44, block, 0.0), jnp.zeros((8, 128), jnp.float32)], axis=1)
        if m:
            wide = pltpu.roll(wide, 44 * m, 1)
        bias = wide if bias is None else bias + wide
        exch_sum = energy if exch_sum is None else exch_sum + energy
    bias, exch_sum = bias[0:2, 0:176], exch_sum[0:2]
    first = lax.broadcasted_iota(jnp.int32, (2, 1), 0) == 0
    root = np.sqrt(np.float32(176))
    coulomb = jnp.sum(bias * bias, axis=1, keepdims=True) / (2.0 * root)
    exchange = -exch_sum / (2.0 * root)
    importance = jnp.sum(fields[...] * bias - 0.5 * bias * bias, axis=1, keepdims=True) / root
    weight = jnp.where(first, log_weight[0], log_weight[1]) + importance - coulomb - exchange
    member = lax.broadcasted_iota(jnp.int32, (2, 128), 1) == jnp.where(
        lax.broadcasted_iota(jnp.int32, (2, 128), 0) == 0, group_of[0], group_of[1]
    )
    group = jnp.sum(jnp.where(member, jnp.exp(weight), 0.0), axis=0, keepdims=True)

    for stage in range(2):
        extent, other = STAGES[stage]
        at, beside = (x, y) if stage == 0 else (z, core)
        group = jnp.broadcast_to(group, (8, 128))
        stage_out[stage] = group
        stage_in[stage, 0] = group
        far_first = sorted(
            ((a, b) for a in range(extent) for b in range(other)),
            key=lambda peer: -min(peer[0], extent - peer[0]) - min(peer[1], other - peer[1]),
        )
        for a, b in far_first[:-1]:
            pltpu.make_async_remote_copy(
                src_ref=stage_out.at[stage], dst_ref=stage_in.at[stage, a + extent * b],
                send_sem=s_send.at[stage], recv_sem=s_recv.at[stage],
                device_id=stage_peer(stage, a, b), device_id_type=MESH,
            ).start()
        if stage == 0:
            bias_out[...] = bias
            for w in range(2):
                scalars_out[w] = jnp.sum(coulomb[w : w + 1])
                scalars_out[2 + w] = jnp.sum(exchange[w : w + 1])
                scalars_out[4 + w] = jnp.sum(weight[w : w + 1])
        everyone = stage_in.at[stage, pl.ds(1, 15)]
        whole = pltpu.make_async_remote_copy(
            src_ref=everyone, dst_ref=everyone, send_sem=s_send.at[stage], recv_sem=s_recv.at[stage],
            device_id=sibling, device_id_type=MESH,
        )
        whole.wait_recv()
        whole.wait_send()
        group = None
        steps_a = [lax.rem(at - a + extent, extent) for a in range(extent)]
        steps_b = [lax.rem(beside - b + other, other) * extent for b in range(other)]
        for b in range(other):
            for a in range(extent):
                term = stage_in[stage, steps_a[a] + steps_b[b], 0:1, :]
                group = term if group is None else group + term
    share_out[...] = (GROUPS * group / jnp.sum(group, axis=1, keepdims=True))[:, 0:GROUPS]

    for step in range(6):
        for side in range(2):
            x_copy(step, side).wait_send()
            near_copy(step, side, core).wait_send()
    for n in range(9):
        across_copy(n).wait_send()
    for slot in range(1, 8):
        for h in range(2):
            g_copy(slot, h).wait_send()
    for copy in returns:
        copy.wait_send()


def hand_out(bias, scalars, share, bias_out, coulomb_out, exchange_out, weight_out, share_out):
    bias_out[...] = bias[...]
    share_out[...] = share[...]
    for w in range(2):
        coulomb_out[w] = scalars[w]
        exchange_out[w] = scalars[2 + w]
        weight_out[w] = scalars[4 + w]


def local(greens, cholesky, fields, log_weight, group_of):
    f32, bf16 = jnp.float32, jnp.bfloat16
    dma = pltpu.SemaphoreType.DMA
    vmem = pl.BlockSpec(memory_space=pltpu.VMEM)
    smem = pl.BlockSpec(memory_space=pltpu.SMEM)
    hbm = pl.BlockSpec(memory_space=pl.ANY)
    bias, scalars, share = pl.pallas_call(
        kernel,
        out_shape=[
            jax.ShapeDtypeStruct((2, 176), f32),
            jax.ShapeDtypeStruct((6,), f32),
            jax.ShapeDtypeStruct((1, GROUPS), f32),
        ],
        in_specs=[hbm, hbm, vmem, smem, smem],
        out_specs=[vmem, smem, vmem],
        scratch_shapes=[
            pltpu.VMEM((4, 100, 2, 1000), bf16),
            pltpu.VMEM((11, 100, 2, 1000), bf16),
            pltpu.VMEM((2, 100, 2, 1000), bf16),
            pltpu.VMEM((2, 100, 1000), bf16),
            pltpu.VMEM((PLANES + 16, 100, 1000), bf16),
            pltpu.VMEM((STREAM * ROWS, 256), f32),
            pltpu.VMEM((STREAM * ROWS, 256), f32),
            pltpu.VMEM((16, 48, 128), f32),
            pltpu.VMEM((16, 8, 128), f32),
            pltpu.VMEM((48, 128), f32),
            pltpu.VMEM((8, 8, 128), f32),
            pltpu.VMEM((8, 8, 128), f32),
            pltpu.VMEM((4, 8, 128), f32),
            pltpu.VMEM((2, 8, 128), f32),
            pltpu.VMEM((2, 16, 8, 128), f32),
            dma((3,)),
            dma((6, 2)),
            dma((6, 2)),
            dma((6, 2)),
            dma((6, 2)),
            dma((9,)),
            dma((9,)),
            dma((9,)),
            dma((8, 2)),
            dma((8, 2)),
            dma((8,)),
            dma((8,)),
            dma((2,)),
            dma((2,)),
        ],
        compiler_params=pltpu.CompilerParams(
            collective_id=0, has_side_effects=True, vmem_limit_bytes=56 * 2**20
        ),
        cost_estimate=pl.CostEstimate(flops=14_080_000_000, bytes_accessed=6_000_000, transcendentals=256),
    )(jnp.transpose(greens, (0, 2, 1, 3)), jnp.transpose(cholesky, (0, 2, 1, 3)), fields, log_weight, group_of)
    pair = jax.ShapeDtypeStruct((2,), f32)
    bias, coulomb, exchange, weight, share = pl.pallas_call(
        hand_out,
        out_shape=[bias, pair, pair, pair, share],
        in_specs=[vmem, smem, vmem],
        out_specs=[vmem, smem, smem, smem, vmem],
    )(bias, scalars, share)
    return bias, coulomb, exchange, weight, share.reshape(GROUPS)


def solution(mesh):
    in_specs = (
        P(("walk", "chol"), None, None, None),
        P("chol", None, None, None),
        P(("walk", "chol"), None),
        P(("walk", "chol")),
        P(("walk", "chol")),
    )
    out_specs = (
        P(("walk", "chol"), None),
        P(("walk", "chol")),
        P(("walk", "chol")),
        P(("walk", "chol")),
        P(),
    )
    return jax.shard_map(local, mesh=mesh, in_specs=in_specs, out_specs=out_specs, check_vma=False)
```

```python
import jax
import jax.numpy as jnp
import numpy as np
from jax import lax
from jax.experimental import pallas as pl
from jax.experimental.pallas import tpu as pltpu
from jax.sharding import PartitionSpec as P

GROUPS = 16
ROWS = 104
STREAM = 8
PLANES = 44
MESH = pl.DeviceIdType.MESH
HIGHEST = lax.Precision.HIGHEST

SLOTS = ((0, 0), (1, 0), (0, -1), (0, 1), (1, -1), (0, 2), (1, 1), (1, -2))
WALKERS = (
    (0, 0), (0, 1), (1, 0), (2, 0), (3, 0), (1, 1), (2, 1), (3, 1),
    (4, 0), (5, 0), (4, 1), (5, 1), (6, 0), (7, 0), (6, 1), (7, 1),
)
QUARTERS = ((0, 1), (3, 6), (5, 7), (2, 4))

STEPS = (
    ((-1, 0), (1, 2)),
    ((-1, 1), (1, 0)),
    ((2, 0), (2, 2)),
    ((-1, 2), (1, 3)),
    ((2, 1), (1, 1)),
    ((-1, 3), (2, 3)),
)
ACROSS = ((0, 0), (0, 1), (1, 0), (1, 1), (2, 0), (2, 1), (3, 0), (4, 0), (4, 1))
STAGES = ((4, 4), (8, 2))
STEP_PLACE = (11, 15, 23, 27, 34, 40)
ACROSS_PLACE = (19, 20, 21, 22, 31, 32, 33, 38, 39)


REPEATS = 30


def task_list():
    walkers = PLANES

    def early(*pairs):
        return [(walkers, 2 * pair) for pair in pairs]

    def blocks(numbers, *pairs):
        return [(8 * number, walkers + 2 * pair) for pair in pairs for number in numbers]

    tasks = blocks((0,), 0, 1, 2, 3) + early(4, 5, 6, 7, 8, 9)
    tasks += blocks((0, 1), 4) + early(10, 12, 11) + blocks((2,), 4)
    tasks += blocks((0, 1, 2), 5) + early(13, 14) + blocks((3,), 4, 5) + early(15)
    tasks += blocks((0, 1, 2), 6) + early(16, 17, 18) + blocks((3,), 6)
    tasks += [(REPEATS, walkers + 2 * pair) for pair in (4, 5, 6)]
    tasks += blocks((0, 1, 2, 3), 7) + [(REPEATS, walkers + 14)] + early(20, 21, 19)
    return tasks + [(walkers + 8, 2 * pair) for pair in (20, 21, 19)]


TASKS = task_list()


def segments(values):
    found, start = [], 0
    while start < len(values):
        end = start + 1
        slope = values[end] - values[start] if end < len(values) else 0
        while end < len(values) and values[end] == values[start] + slope * (end - start):
            end += 1
        found.append((end, start, values[start], slope))
        start = end
    return found


def lookup(values, t):
    def pick(found):
        if len(found) == 1:
            _, start, value, slope = found[0]
            return value + (t - start) * slope if slope else jnp.int32(value)
        half = len(found) // 2
        return jnp.where(t < found[half - 1][0], pick(found[:half]), pick(found[half:]))

    return pick(segments(values))


def device(x, y, z, core):
    return {"walk": (y * 2 + lax.div(z, 4)) * 2 + core, "chol": lax.rem(z, 4) * 4 + x}


def kernel(
    greens, cholesky, fields, log_weight, group_of,
    bias_out, scalars_out, share_out,
    raw_first, raw_c, raw_g, others, items, prods_a, prods_b, bias_rows, exch, order,
    back, back_in, combined, stage_out, stage_in,
    local_sem, x_send, x_recv, near_send, near_recv, y_send, y_recv, far_recv,
    g_send, g_recv, b_send, b_recv, s_send, s_recv,
):
    wi, ci = lax.axis_index("walk"), lax.axis_index("chol")
    core = lax.rem(wi, 2)
    y = lax.div(wi, 4)
    z_lo = lax.div(ci, 4)
    z = lax.rem(lax.div(wi, 2), 2) * 4 + z_lo
    x = lax.rem(ci, 4)
    spin = lax.div(y, 2)
    mate = 3 - y
    odd = lax.rem(y, 2)
    neighbour = y + 1 - 2 * odd
    sends_across = core == odd

    def at_x(offset):
        return lax.rem(x + offset + 4, 4)

    def at_z(offset):
        return lax.rem(z + offset + 8, 8)

    def stage_peer(stage, a, b):
        if stage == 0:
            return device(xs[a], ys[b], z, core)
        return device(x, y, zs[a], cores[b])

    xs = [at_x(a) for a in range(4)]
    ys = [lax.rem(y + b, 4) for b in range(4)]
    zs = [at_z(a) for a in range(8)]
    cores = [core, 1 - core]

    own_c = pltpu.make_async_copy(cholesky, raw_c, local_sem.at[0])
    own_g = pltpu.make_async_copy(greens, raw_g, local_sem.at[1])
    first_plane = 3 * odd + 4 * core
    first_c = pltpu.make_async_copy(cholesky.at[pl.ds(first_plane, 4)], raw_first, local_sem.at[2])
    own_g.start()
    first_c.start()
    own_c.start()

    barrier = pltpu.get_barrier_semaphore()

    def greet(peer):
        pl.semaphore_signal(barrier, inc=1, device_id=peer, device_id_type=MESH)

    sibling = device(x, y, z, 1 - core)
    to_side = (device(at_x(1), y, z, core), device(at_x(-1), y, z, core))
    up, down = device(x, y, at_z(1), core), device(x, y, at_z(-1), core)
    for peer in (*to_side, up, down, sibling, device(x, neighbour, z, core), device(x, mate, z, core)):
        greet(peer)

    def plane_of(i, c):
        first = 3 * odd + 4 * c
        return first + odd + i if i < 3 else first + 3 * (1 - odd)

    def place(step, side, c):
        return STEP_PLACE[step] + side * 2 + c

    lanes = lax.broadcasted_iota(jnp.int32, (1, 128), 1)
    rows = [(i, x * 11 + i) for i in range(11)]
    for step in range(6):
        for side in range(2):
            home, i = STEPS[step][side]
            for c in range(2):
                rows.append((place(step, side, c), at_x(home) * 11 + plane_of(i, c)))
    for n, (step, side) in enumerate(ACROSS):
        home, i = STEPS[step][side]
        rows.append((ACROSS_PLACE[n], at_x(home) * 11 + 8 * (1 - odd) + i))
    rows.append((44, 44))
    def by_spin(pair):
        apart = jnp.swapaxes(pair, 0, 1)
        low = spin == 0
        return jnp.where(low, apart[0], apart[1]), jnp.where(low, apart[1], apart[0])

    own_g.wait()
    for h in range(2):
        items[PLANES + h], others[h] = by_spin(raw_g[h])
    first_c.wait()
    for i in range(4):
        items[first_plane + i] = by_spin(raw_first[i])[0]
    pl.semaphore_wait(barrier, 7)

    def x_copy(step, side):
        home, i = STEPS[step][side]
        if home == 2:
            before = STEPS.index(next(s for s in STEPS if s[side] == ((-1, 1)[side], i)))
            src = items.at[place(before, side, core)]
        else:
            src = items.at[plane_of(i, core)]
        return pltpu.make_async_remote_copy(
            src_ref=src, dst_ref=items.at[place(step, side, core)],
            send_sem=x_send.at[step, side], recv_sem=x_recv.at[step, side],
            device_id=to_side[side], device_id_type=MESH,
        )

    def near_copy(step, side, c):
        ref = items.at[place(step, side, c)]
        return pltpu.make_async_remote_copy(
            src_ref=ref, dst_ref=ref, send_sem=near_send.at[step, side], recv_sem=near_recv.at[step, side],
            device_id=sibling, device_id_type=MESH,
        )

    def across_copy(n):
        step, side = ACROSS[n]
        return pltpu.make_async_remote_copy(
            src_ref=items.at[place(step, side, core)], dst_ref=items.at[ACROSS_PLACE[n]],
            send_sem=y_send.at[n], recv_sem=y_recv.at[n],
            device_id=device(x, neighbour, z, core), device_id_type=MESH,
        )

    def onward_copy(n):
        ref = items.at[ACROSS_PLACE[n]]
        return pltpu.make_async_remote_copy(
            src_ref=ref, dst_ref=ref, send_sem=y_send.at[n], recv_sem=far_recv.at[n],
            device_id=sibling, device_id_type=MESH,
        )

    def g_copy(slot, h):
        if slot < 4:
            src = others.at[h] if slot == 1 else items.at[PLANES + h]
        else:
            src = items.at[PLANES + WALKERS.index(({4: 1, 5: 3, 6: 1, 7: 4}[slot], h))]
        peer = device(x, mate, z, core) if slot == 1 else up if slot in (2, 4, 7) else down
        return pltpu.make_async_remote_copy(
            src_ref=src, dst_ref=items.at[PLANES + WALKERS.index((slot, h))],
            send_sem=g_send.at[slot, h], recv_sem=g_recv.at[slot, h],
            device_id=peer, device_id_type=MESH,
        )

    def x_start(step):
        for side in range(2):
            x_copy(step, side).start()

    def x_arrived(step):
        for side in range(2):
            x_copy(step, side).wait_recv()
            near_copy(step, side, core).start()

        @pl.when(sends_across)
        def _():
            for n, (s, _side) in enumerate(ACROSS):
                if s == step:
                    across_copy(n).start()

    def across_arrived(numbers):
        @pl.when(jnp.logical_not(sends_across))
        def _():
            for n in numbers:
                across_copy(n).wait_recv()
                onward_copy(n).start()

    def near_arrived(*steps):
        for step in steps:
            for side in range(2):
                near_copy(step, side, 1 - core).wait_recv()

    def onward_arrived(numbers):
        @pl.when(sends_across)
        def _():
            for n in numbers:
                onward_copy(n).wait_recv()

    def begin(step):
        g_copy(1, step).start()
        x_start(step)
        g_copy(2, step).start()
        g_copy(3, step).start()

    begin(0)
    begin(1)
    own_c.wait()

    def take(i, _):
        at = lax.rem(first_plane + 4 + i, 11)
        items[at] = by_spin(raw_c[at])[0]
        return 0

    lax.fori_loop(0, 7, take, 0)
    order[...] = jnp.zeros_like(order)
    for at, row in rows:
        order[at : at + 1, :] = (lanes == row).astype(jnp.float32)
    bias_rows[...] = jnp.zeros_like(bias_rows)
    exch[...] = jnp.zeros_like(exch)
    prods_b[...] = jnp.zeros_like(prods_b)
    back[...] = jnp.zeros_like(back)

    row = lax.broadcasted_iota(jnp.int32, (8, 128), 0)
    col = lax.broadcasted_iota(jnp.int32, (8, 128), 1)
    tile = lax.div(col, 8)
    diagonal = jnp.logical_and(row == lax.rem(col, 8), col < ROWS)
    gap = jnp.zeros((28, 1000), jnp.bfloat16)

    def task(t):
        return lookup([a for a, _ in TASKS], t), lookup([b for _, b in TASKS], t)

    def product(t, buf):
        first, pair = task(t)
        lhs = [part for i in range(STREAM) for part in (items[first + i], gap[: ROWS - 100])]
        rhs = [items[pair], gap, items[pair + 1], gap]
        buf[...] = lax.dot_general(
            jnp.concatenate(lhs, axis=0), jnp.concatenate(rhs, axis=0), (((1,), (1,)), ((), ())),
            preferred_element_type=jnp.float32,
        )

    def reduce(t, buf):
        first, pair = task(t)
        streams_walkers = first >= PLANES
        for h in range(2):
            for g in range(STREAM):
                walker = jnp.where(streams_walkers, first + g, pair + h) - PLANES
                plane = jnp.where(streams_walkers, pair + h, first + g)
                p = buf[g * ROWS : (g + 1) * ROWS, h * 128 : (h + 1) * 128]
                turned = p.T
                q = p[:, :ROWS] * turned[:ROWS, :]
                part = jnp.sum(q.reshape(ROWS // 8, 8, ROWS), axis=0)
                if g < 2:
                    part = jnp.where(first == REPEATS, 0.0, part)
                exch[walker, :, 0:ROWS] += part
                d = p[0:8]
                for r in range(1, ROWS // 8):
                    d = jnp.where(tile == r, p[r * 8 : r * 8 + 8], d)
                d = jnp.where(diagonal, d, 0.0)
                bias_rows[walker, pl.ds(plane, 1), :] = jnp.sum(d, axis=0, keepdims=True)

    def before(t):
        def at(when, work):
            pl.when(t == when)(work)

        def walker(slot, h, *onward):
            g_copy(slot, h).wait_recv()
            for later in onward:
                g_copy(later, h).start()

        def first(h):
            x_arrived(h)
            x_start(h + 2)
            walker(3, h, 5)
            walker(1, h, 4)
            walker(2, h)

        def second():
            near_arrived(0, 1)
            across_arrived((0,))

        def third():
            x_arrived(2)
            x_start(4)
            walker(4, 0, 7, 6)
            walker(5, 0)
            across_arrived((1, 2))

        def fourth():
            near_arrived(2)
            onward_arrived((1, 2))
            across_arrived((3,))

        def fifth():
            x_arrived(3)
            x_start(5)
            walker(4, 1, 7, 6)
            walker(5, 1)
            across_arrived((4,))

        def sixth():
            x_arrived(4)
            walker(6, 0)
            walker(7, 0)
            across_arrived((5, 6))

        def seventh():
            near_arrived(4)
            onward_arrived((5, 6))

        def eighth():
            x_arrived(5)
            walker(6, 1)
            walker(7, 1)

        def split(when, early, late):
            lax.cond(t < when, early, late)

        def run(*work):
            def go():
                for when, what in work:
                    at(when, what)
            return go

        split(
            16,
            lambda: split(
                6,
                run((0, lambda: first(0)), (2, lambda: first(1)), (4, second)),
                lambda: split(
                    12,
                    run((8, lambda: onward_arrived((0,))), (10, third)),
                    run((12, fourth), (14, lambda: onward_arrived((3,)))),
                ),
            ),
            lambda: split(
                28,
                lambda: split(
                    22,
                    run((16, fifth), (18, lambda: near_arrived(3)), (20, lambda: onward_arrived((4,)))),
                    run((24, sixth), (26, seventh)),
                ),
                lambda: split(
                    38,
                    run((34, eighth), (36, lambda: across_arrived((7, 8)))),
                    run((38, lambda: near_arrived(5)), (40, lambda: onward_arrived((7, 8)))),
                ),
            ),
        )

    def body(k, _):
        before(2 * k)

        product(2 * k, prods_a)
        reduce(jnp.maximum(2 * k - 1, 0), prods_b)
        product(2 * k + 1, prods_b)
        reduce(2 * k, prods_a)

        return 0

    lax.fori_loop(0, len(TASKS) // 2, body, 0)
    product(jnp.int32(len(TASKS) - 1), prods_a)
    reduce(jnp.int32(len(TASKS) - 2), prods_b)
    reduce(jnp.int32(len(TASKS) - 1), prods_a)

    for w in range(16):
        bias_rows[w, 44:45, :] = jnp.sum(exch[w], axis=0, keepdims=True)
    wide = jnp.dot(
        bias_rows[...].reshape(16 * 48, 128), jnp.ones((128, 128), jnp.float32),
        precision=HIGHEST, preferred_element_type=jnp.float32,
    ).reshape(16, 48, 128)
    sums = [jnp.sum(wide[w] * order[...], axis=0, keepdims=True) for w in range(16)]
    for slot in range(8):
        for h in range(2):
            back[slot, h : h + 1] = sums[WALKERS.index((slot, h))]
    returns = []
    for slot, (other, offset) in reversed(tuple(enumerate(SLOTS))):
        if slot:
            copy = pltpu.make_async_remote_copy(
                src_ref=back.at[slot], dst_ref=back_in.at[slot], send_sem=b_send.at[slot], recv_sem=b_recv.at[slot],
                device_id=device(x, mate if other else y, at_z(offset), core), device_id_type=MESH,
            )
            copy.start()
            returns.append(copy)
    for copy in returns:
        copy.wait_recv()
    for quarter, (s, t) in enumerate(QUARTERS):
        combined[quarter] = (back[0] if s == 0 else back_in[s]) + back_in[t]
    lane = lax.broadcasted_iota(jnp.int32, (8, 128), 1)
    bias, exch_sum = None, None
    for m in range(4):
        block = combined[lax.rem(z_lo - m + 4, 4)]
        energy = jnp.sum(jnp.where(lane == 44, block, 0.0), axis=1, keepdims=True)
        wide = jnp.concatenate([jnp.where(lane < 44, block, 0.0), jnp.zeros((8, 128), jnp.float32)], axis=1)
        if m:
            wide = pltpu.roll(wide, 44 * m, 1)
        bias = wide if bias is None else bias + wide
        exch_sum = energy if exch_sum is None else exch_sum + energy
    bias, exch_sum = bias[0:2, 0:176], exch_sum[0:2]
    first = lax.broadcasted_iota(jnp.int32, (2, 1), 0) == 0
    root = np.sqrt(np.float32(176))
    coulomb = jnp.sum(bias * bias, axis=1, keepdims=True) / (2.0 * root)
    exchange = -exch_sum / (2.0 * root)
    importance = jnp.sum(fields[...] * bias - 0.5 * bias * bias, axis=1, keepdims=True) / root
    weight = jnp.where(first, log_weight[0], log_weight[1]) + importance - coulomb - exchange
    member = lax.broadcasted_iota(jnp.int32, (2, 128), 1) == jnp.where(
        lax.broadcasted_iota(jnp.int32, (2, 128), 0) == 0, group_of[0], group_of[1]
    )
    group = jnp.sum(jnp.where(member, jnp.exp(weight), 0.0), axis=0, keepdims=True)

    for stage in range(2):
        extent, other = STAGES[stage]
        at, beside = (x, y) if stage == 0 else (z, core)
        group = jnp.broadcast_to(group, (8, 128))
        stage_out[stage] = group
        stage_in[stage, 0] = group
        far_first = sorted(
            ((a, b) for a in range(extent) for b in range(other)),
            key=lambda peer: -min(peer[0], extent - peer[0]) - min(peer[1], other - peer[1]),
        )
        for a, b in far_first[:-1]:
            pltpu.make_async_remote_copy(
                src_ref=stage_out.at[stage], dst_ref=stage_in.at[stage, a + extent * b],
                send_sem=s_send.at[stage], recv_sem=s_recv.at[stage],
                device_id=stage_peer(stage, a, b), device_id_type=MESH,
            ).start()
        if stage == 0:
            bias_out[...] = bias
            for w in range(2):
                scalars_out[w] = jnp.sum(coulomb[w : w + 1])
                scalars_out[2 + w] = jnp.sum(exchange[w : w + 1])
                scalars_out[4 + w] = jnp.sum(weight[w : w + 1])
        everyone = stage_in.at[stage, pl.ds(1, 15)]
        whole = pltpu.make_async_remote_copy(
            src_ref=everyone, dst_ref=everyone, send_sem=s_send.at[stage], recv_sem=s_recv.at[stage],
            device_id=sibling, device_id_type=MESH,
        )
        whole.wait_recv()
        whole.wait_send()
        group = None
        steps_a = [lax.rem(at - a + extent, extent) for a in range(extent)]
        steps_b = [lax.rem(beside - b + other, other) * extent for b in range(other)]
        for b in range(other):
            for a in range(extent):
                term = stage_in[stage, steps_a[a] + steps_b[b], 0:1, :]
                group = term if group is None else group + term
    share_out[...] = (GROUPS * group / jnp.sum(group, axis=1, keepdims=True))[:, 0:GROUPS]

    for step in range(6):
        for side in range(2):
            x_copy(step, side).wait_send()
            near_copy(step, side, core).wait_send()
    for n in range(9):
        across_copy(n).wait_send()
    for slot in range(1, 8):
        for h in range(2):
            g_copy(slot, h).wait_send()
    for copy in returns:
        copy.wait_send()


def hand_out(bias, scalars, share, bias_out, coulomb_out, exchange_out, weight_out, share_out):
    bias_out[...] = bias[...]
    share_out[...] = share[...]
    for w in range(2):
        coulomb_out[w] = scalars[w]
        exchange_out[w] = scalars[2 + w]
        weight_out[w] = scalars[4 + w]


def local(greens, cholesky, fields, log_weight, group_of):
    f32, bf16 = jnp.float32, jnp.bfloat16
    dma = pltpu.SemaphoreType.DMA
    vmem = pl.BlockSpec(memory_space=pltpu.VMEM)
    smem = pl.BlockSpec(memory_space=pltpu.SMEM)
    hbm = pl.BlockSpec(memory_space=pl.ANY)
    bias, scalars, share = pl.pallas_call(
        kernel,
        out_shape=[
            jax.ShapeDtypeStruct((2, 176), f32),
            jax.ShapeDtypeStruct((6,), f32),
            jax.ShapeDtypeStruct((1, GROUPS), f32),
        ],
        in_specs=[hbm, hbm, vmem, smem, smem],
        out_specs=[vmem, smem, vmem],
        scratch_shapes=[
            pltpu.VMEM((4, 100, 2, 1000), bf16),
            pltpu.VMEM((11, 100, 2, 1000), bf16),
            pltpu.VMEM((2, 100, 2, 1000), bf16),
            pltpu.VMEM((2, 100, 1000), bf16),
            pltpu.VMEM((PLANES + 16, 100, 1000), bf16),
            pltpu.VMEM((STREAM * ROWS, 256), f32),
            pltpu.VMEM((STREAM * ROWS, 256), f32),
            pltpu.VMEM((16, 48, 128), f32),
            pltpu.VMEM((16, 8, 128), f32),
            pltpu.VMEM((48, 128), f32),
            pltpu.VMEM((8, 8, 128), f32),
            pltpu.VMEM((8, 8, 128), f32),
            pltpu.VMEM((4, 8, 128), f32),
            pltpu.VMEM((2, 8, 128), f32),
            pltpu.VMEM((2, 16, 8, 128), f32),
            dma((3,)),
            dma((6, 2)),
            dma((6, 2)),
            dma((6, 2)),
            dma((6, 2)),
            dma((9,)),
            dma((9,)),
            dma((9,)),
            dma((8, 2)),
            dma((8, 2)),
            dma((8,)),
            dma((8,)),
            dma((2,)),
            dma((2,)),
        ],
        compiler_params=pltpu.CompilerParams(
            collective_id=0, has_side_effects=True, vmem_limit_bytes=56 * 2**20
        ),
        cost_estimate=pl.CostEstimate(flops=14_080_000_000, bytes_accessed=6_000_000, transcendentals=256),
    )(jnp.transpose(greens, (0, 2, 1, 3)), jnp.transpose(cholesky, (0, 2, 1, 3)), fields, log_weight, group_of)
    pair = jax.ShapeDtypeStruct((2,), f32)
    bias, coulomb, exchange, weight, share = pl.pallas_call(
        hand_out,
        out_shape=[bias, pair, pair, pair, share],
        in_specs=[vmem, smem, vmem],
        out_specs=[vmem, smem, smem, smem, vmem],
    )(bias, scalars, share)
    return bias, coulomb, exchange, weight, share.reshape(GROUPS)


def solution(mesh):
    in_specs = (
        P(("walk", "chol"), None, None, None),
        P("chol", None, None, None),
        P(("walk", "chol"), None),
        P(("walk", "chol")),
        P(("walk", "chol")),
    )
    out_specs = (
        P(("walk", "chol"), None),
        P(("walk", "chol")),
        P(("walk", "chol")),
        P(("walk", "chol")),
        P(),
    )
    return jax.shard_map(local, mesh=mesh, in_specs=in_specs, out_specs=out_specs, check_vma=False)
```
